128 devices in a mesh: frame: 16 (over y_hi, x, core), patch: 8 (over z, y_lo).
Axes of the slice: x: 4, y: 4 (y_hi: 2, y_lo: 2; y = y_hi * 2 + y_lo), z: 4, core: 2. Of those that a mesh axis runs over, the one named last changes fastest.
Arguments:
- video_tokens: bfloat16 [32, 512, 3072], P('frame', 'patch'), may hold values from -6 to 6
- spatial_query: bfloat16 [3072, 3072], P('frame', 'patch')
- spatial_key: bfloat16 [3072, 3072], P('frame', 'patch')
- spatial_value: bfloat16 [3072, 3072], P('frame', 'patch'), may hold values from -0.109375 to 0.109375
- spatial_proj: bfloat16 [3072, 3072], P('patch'), may hold values from -0.109375 to 0.109375
- temporal_query: bfloat16 [3072, 3072], P('frame', 'patch')
- temporal_key: bfloat16 [3072, 3072], P('frame', 'patch')
- temporal_value: bfloat16 [3072, 3072], P('frame', 'patch'), may hold values from -0.109375 to 0.109375
- temporal_proj: bfloat16 [3072, 3072], P('patch'), may hold values from -0.109375 to 0.109375
- modulation: float32 [4, 3072], replicated, may hold values from -3 to 3
- branch_gates: float32 [2, 3072], replicated, may hold values from 2 to 20
Outputs:
- after_spatial: bfloat16 [32, 512, 3072], P('frame', 'patch')
- after_temporal: bfloat16 [32, 512, 3072], P('frame', 'patch')
The draws below stay inside these ranges and needn't reach their ends.
All inputs are finite; a program needn't handle non-finite values.
Results may differ from the reference program's by a relative error of at most 0.04.
Values may be sent and summed in bfloat16 or wider, within the bound.
A program may use at most 64 MiB of HBM per device.

```python
import math
import jax
import jax.numpy as jnp
from jax import lax

D = 3072
HEADS = 24
FRAMES = 32
PATCHES = 512
N_PATCH = 8


def draw_spatial_query(key, part):
    key = jax.random.fold_in(key, 11)
    noise = jax.random.normal(key, (D, D), jnp.float32) * D ** (-0.5)
    return noise.astype(jnp.bfloat16)


def draw_spatial_key(key, part):
    key = jax.random.fold_in(key, 12)
    noise = jax.random.normal(key, (D, D), jnp.float32) * D ** (-0.5)
    return noise.astype(jnp.bfloat16)


def draw_temporal_query(key, part):
    key = jax.random.fold_in(key, 13)
    noise = jax.random.normal(key, (D, D), jnp.float32) * D ** (-0.5)
    return (1.7 * noise).astype(jnp.bfloat16)


def draw_temporal_key(key, part):
    key = jax.random.fold_in(key, 14)
    noise = jax.random.normal(key, (D, D), jnp.float32) * D ** (-0.5)
    return (1.7 * noise).astype(jnp.bfloat16)


def level_of(stream_key, shape, cuts, least, largest):
    loudness = 1.0
    for axis_at, parts in cuts:
        draws = jax.random.uniform(jax.random.fold_in(jax.random.fold_in(stream_key, 6), axis_at), (parts,), jnp.float32, least / len(cuts), largest / len(cuts))
        loudness = loudness * jnp.repeat(jnp.exp(draws), shape[axis_at] // parts).reshape((-1,) + (1,) * (len(shape) - 1 - axis_at))
    return loudness


def scatter_about(rng, extent, deviation, limit, cuts=(), held_as=jnp.bfloat16):
    factor_of = level_of(rng, extent, cuts, -0.22, 0.18) if cuts else 1.0
    entries = jax.random.normal(rng, extent, jnp.float32) * deviation * factor_of
    return jnp.minimum(jnp.maximum(entries, -limit), limit).astype(held_as)


def setup_inputs(seed: int = 0) -> dict:
    arg_keys = jax.random.split(jax.random.key(seed), 12)
    video_tokens = scatter_about(arg_keys[0], (FRAMES, PATCHES, D), 1.0, 6.0, ((0, 16), (1, 8)))
    spatial_query = draw_spatial_query(jax.random.fold_in(arg_keys[11], 71), 0)
    spatial_key = draw_spatial_key(jax.random.fold_in(arg_keys[11], 71), 0)
    spatial_value = scatter_about(arg_keys[3], (D, D), D ** -0.5, 0.109375, ((0, 16), (1, 8)))
    spatial_proj = scatter_about(arg_keys[4], (D, D), D ** -0.5, 0.109375, ((0, 8),))
    temporal_query = draw_temporal_query(jax.random.fold_in(arg_keys[11], 71), 0)
    temporal_key = draw_temporal_key(jax.random.fold_in(arg_keys[11], 71), 0)
    temporal_value = scatter_about(arg_keys[7], (D, D), D ** -0.5, 0.109375, ((0, 16), (1, 8)))
    temporal_proj = scatter_about(arg_keys[8], (D, D), D ** -0.5, 0.109375, ((0, 8),))
    modulation = scatter_about(arg_keys[9], (4, D), 0.5, 3.0, (), jnp.float32)
    branch_gates = jnp.clip(jnp.exp(jax.random.uniform(arg_keys[10], (2, D), jnp.float32, math.log(2.0), math.log(20.0))), 2.0, 20.0)
    return {"video_tokens": video_tokens, "spatial_query": spatial_query, "spatial_key": spatial_key, "spatial_value": spatial_value, "spatial_proj": spatial_proj, "temporal_query": temporal_query, "temporal_key": temporal_key, "temporal_value": temporal_value, "temporal_proj": temporal_proj, "modulation": modulation, "branch_gates": branch_gates}


EPS = 1e-06

def norm_modulate(tokens, shift, scale):
    values = tokens.astype(jnp.float32)
    center = values - lax.optimization_barrier(jnp.mean(values, axis=-1, keepdims=True))
    spread = lax.optimization_barrier(jnp.mean(center * center, axis=-1, keepdims=True))
    return (center * lax.rsqrt(spread + EPS) * (1.0 + scale) + shift).astype(jnp.bfloat16)

def project_rows(tokens, matrix):
    flat = tokens.reshape(-1, tokens.shape[-1])
    result = jnp.dot(flat, matrix, preferred_element_type=jnp.float32).astype(jnp.bfloat16)
    return result.reshape(tokens.shape[:-1] + (matrix.shape[1],))

def softmax_rows(scores):
    top = lax.optimization_barrier(jnp.max(scores, axis=-1, keepdims=True))
    expon = jnp.exp(scores - top)
    return (expon / lax.optimization_barrier(jnp.sum(expon, axis=-1, keepdims=True))).astype(jnp.bfloat16)

def spatial_frame(inputs):
    query_rows, key_rows, value_rows = inputs
    shape = (query_rows.shape[0], HEADS, D // HEADS)
    queries = query_rows.reshape(shape).astype(jnp.float32)
    key_vals = key_rows.reshape(shape).astype(jnp.float32)
    value_vals = value_rows.reshape(shape).astype(jnp.float32)
    scores = jnp.einsum('qhc,khc->hqk', queries, key_vals) * float(D // HEADS) ** (-0.5)
    weights = softmax_rows(scores).astype(jnp.float32)
    attended = jnp.einsum('hqk,khc->qhc', weights, value_vals).astype(jnp.bfloat16)
    return attended.reshape(query_rows.shape[0], D)

def temporal_attend(query_rows, key_rows, value_rows):
    shape = query_rows.shape[:2] + (HEADS, D // HEADS)
    queries = query_rows.reshape(shape).astype(jnp.float32)
    key_vals = key_rows.reshape(shape).astype(jnp.float32)
    value_vals = value_rows.reshape(shape).astype(jnp.float32)
    scores = jnp.einsum('qbhc,kbhc->bhqk', queries, key_vals) * float(D // HEADS) ** (-0.5)
    weights = softmax_rows(scores).astype(jnp.float32)
    attended = jnp.einsum('bhqk,kbhc->qbhc', weights, value_vals).astype(jnp.bfloat16)
    return attended.reshape(query_rows.shape[:2] + (D,))

def project_out(attended, proj):
    group_cols = D // N_PATCH
    flat = attended.reshape(-1, D)
    total = jnp.zeros((flat.shape[0], D), jnp.float32)
    for group in range(N_PATCH):
        lower = group * group_cols
        term = jnp.dot(flat[:, lower:lower + group_cols], proj[lower:lower + group_cols], preferred_element_type=jnp.float32)
        total = total + lax.optimization_barrier(term.astype(jnp.bfloat16)).astype(jnp.float32)
    rounded = lax.optimization_barrier(total.astype(jnp.bfloat16)).astype(jnp.float32)
    return rounded.reshape(attended.shape)

def reference(video_tokens, spatial_query, spatial_key, spatial_value, spatial_proj, temporal_query, temporal_key, temporal_value, temporal_proj, modulation, branch_gates):
    normed = norm_modulate(video_tokens, modulation[0], modulation[1])
    query_rows = project_rows(normed, spatial_query)
    key_rows = project_rows(normed, spatial_key)
    value_rows = project_rows(normed, spatial_value)
    attended = lax.map(spatial_frame, (query_rows, key_rows, value_rows))
    spatial_out = project_out(attended, spatial_proj)
    after_spatial = (video_tokens.astype(jnp.float32) + branch_gates[0] * spatial_out).astype(jnp.bfloat16)
    normed_next = norm_modulate(after_spatial, modulation[2], modulation[3])
    query_next = project_rows(normed_next, temporal_query)
    key_next = project_rows(normed_next, temporal_key)
    value_next = project_rows(normed_next, temporal_value)
    attended_next = temporal_attend(query_next, key_next, value_next)
    temporal_out = project_out(attended_next, temporal_proj)
    after_temporal = (after_spatial.astype(jnp.float32) + branch_gates[1] * temporal_out).astype(jnp.bfloat16)
    return (after_spatial, after_temporal)
```

```python
import functools

import jax
import jax.numpy as jnp
from jax import lax
from jax.experimental import pallas as pl
from jax.experimental.pallas import tpu as pltpu
from jax.sharding import PartitionSpec as P

D = 3072
HEAD = 128
COLS = 384
HALF = D // 2
EPS = 1e-06
MESH = pl.DeviceIdType.MESH
BF16 = jnp.bfloat16
F32 = jnp.float32


def place():
    f = lax.axis_index("frame")
    p = lax.axis_index("patch")
    return f, p, lax.rem(lax.div(f, 2), 4), lax.div(f, 8), lax.div(p, 2), lax.rem(p, 2), lax.rem(f, 2)


def device(x, y_hi, y_lo, z, core):
    return ((y_hi * 4 + x) * 2 + core, z * 2 + y_lo)


def remote(src, dst, send, recv, to):
    return pltpu.make_async_remote_copy(
        src_ref=src, dst_ref=dst, send_sem=send, recv_sem=recv, device_id=to, device_id_type=MESH
    )


class Sends:
    def __init__(self, sems):
        self.sems = sems
        self.used = 0
        self.open = []

    def start(self, src, dst, recv, to, like, when=None):
        at = self.used
        self.used += 1
        self.open.append((at, like, when))
        remote(src, dst, self.sems.at[at], recv, to).start()

    def finish(self, to):
        def drain(group):
            for at, like, _ in group:
                remote(like, like, self.sems.at[at], self.sems.at[at], to).wait_send()

        conditions = []
        for _, _, when in self.open:
            if not any(when is other for other in conditions):
                conditions.append(when)
        for condition in conditions:
            group = [copy for copy in self.open if copy[2] is condition]
            if condition is None:
                drain(group)
            else:
                pl.when(condition)(functools.partial(drain, group))


def arrived(dst, recv, to):
    remote(dst, dst, recv, recv, to).wait_recv()


def normed(values, shift, scale):
    center = values - jnp.mean(values, axis=-1, keepdims=True)
    spread = jnp.mean(center * center, axis=-1, keepdims=True)
    return (center * lax.rsqrt(spread + EPS) * (1.0 + scale) + shift).astype(BF16)


def heads_of(qkv_ref, att_ref, load, store, mask):
    for h in range(3):
        q = load(h * HEAD)
        k = load(COLS + h * HEAD)
        v = load(2 * COLS + h * HEAD)
        s = lax.dot_general(q, k, (((1,), (1,)), ((), ())), preferred_element_type=F32)
        s = s * (float(HEAD) ** -0.5)
        if mask is not None:
            s = jnp.where(mask, s, -1e30)
        e = jnp.exp(s - jnp.max(s, axis=-1, keepdims=True))
        total = jnp.sum(e, axis=-1, keepdims=True)
        o = jnp.dot(e.astype(BF16), v, preferred_element_type=F32) / total
        store(h * HEAD, o.astype(BF16))


def spatial_kernel(
    x_ref, wq, wk, wv, proj_ref, mod_ref, gate_ref,
    after_ref, next_ref,
    nst, wst, tok, wb, pb, qkv, att, psend, rs, fin, hb,
    send_sem, trecv, wrecv, rrecv, misc, local_sem,
):
    f, p, x, yh, z, yl, c = place()
    root = c == yl
    leaf = c != yl
    sib = device(x, yh, yl, z, 1 - c)
    pair = device(x, yh, 1 - yl, z, c)
    xs = [device(lax.rem(x + k, 4), yh, yl, z, c) for k in (1, 3, 2)]
    ys = [
        device(x, yh, 1 - yl, z, c),
        device(x, 1 - yh, 1 - yl, z, c),
        device(x, 1 - yh, yl, z, c),
    ]
    zs = [device(x, yh, yl, lax.rem(z + k, 4), c) for k in (1, 3, 2)]
    sends = Sends(send_sem)

    def fb(y_hi, x_at, core):
        return (y_hi * 4 + x_at) * 2 + core

    barrier = pltpu.get_barrier_semaphore()
    for to in [sib] + xs + ys + zs:
        pl.semaphore_signal(barrier, inc=1, device_id=to, device_id_type=MESH)
    wst[:, 0:COLS] = wq[...]
    wst[:, COLS : 2 * COLS] = wk[...]
    wst[:, 2 * COLS :] = wv[...]
    pl.semaphore_wait(barrier, 10)

    my_proj = pltpu.make_async_copy(
        proj_ref.at[:, pl.ds(pl.multiple_of(c * HALF, HALF), HALF)], pb.at[yl], local_sem.at[0]
    )
    my_proj.start()
    w_local = pltpu.make_async_copy(wst, wb.at[f], local_sem.at[1])
    t_local = pltpu.make_async_copy(nst, tok.at[p], local_sem.at[2])

    @pl.when(leaf)
    def _():
        sends.start(wst, wb.at[f], wrecv.at[f], sib, wst, leaf)

    @pl.when(root)
    def _():
        w_local.start()
        for to in xs:
            sends.start(wst, wb.at[f], wrecv.at[f], to, wst, root)
        for to in ys:
            sends.start(wst, wb.at[f], wrecv.at[f], to, wst, root)

    for i in range(2):
        for r in range(0, 64, 32):
            nst[i, r : r + 32] = normed(
                x_ref[i, r : r + 32].astype(F32), mod_ref[0:1], mod_ref[1:2]
            )

    @pl.when(leaf)
    def _():
        sends.start(nst, tok.at[p], trecv.at[p], pair, nst, leaf)

    @pl.when(root)
    def _():
        t_local.start()
        for to in zs:
            sends.start(nst, tok.at[p], trecv.at[p], to, nst, root)
        sends.start(nst, tok.at[p], trecv.at[p], sib, nst, root)
        b = fb(yh, x, 1 - c)
        arrived(wb.at[b], wrecv.at[b], sib)
        for to in ys + xs:
            sends.start(wb.at[b], wb.at[b], wrecv.at[b], to, wst, root)
        q = z * 2 + 1 - yl
        arrived(tok.at[q], trecv.at[q], sib)
        for to in zs:
            sends.start(tok.at[q], tok.at[q], trecv.at[q], to, nst, root)
        sends.start(tok.at[q], tok.at[q], trecv.at[q], sib, nst, root)
        for k in (1, 3, 2):
            b2 = fb(yh, lax.rem(x + k, 4), c)
            arrived(wb.at[b2], wrecv.at[b2], sib)
            for to in ys:
                sends.start(wb.at[b2], wb.at[b2], wrecv.at[b2], to, wst, root)
        b3 = fb(1 - yh, x, 1 - c)
        arrived(wb.at[b3], wrecv.at[b3], sib)
        for to in xs:
            sends.start(wb.at[b3], wb.at[b3], wrecv.at[b3], to, wst, root)

    @pl.when(leaf)
    def _():
        for yh2 in range(2):
            b4 = fb(yh2, x, 1 - c)
            arrived(wb.at[b4], wrecv.at[b4], sib)
            for to in xs:
                sends.start(wb.at[b4], wb.at[b4], wrecv.at[b4], to, wst, leaf)

    my_proj.wait()
    sends.start(pb.at[yl], pb.at[yl], misc.at[0], pair, pb.at[0])

    @pl.when(root)
    def _():
        for k in (1, 3, 2):
            for y2 in range(2):
                s = lax.rem(z + k, 4) * 2 + y2
                arrived(tok.at[s], trecv.at[s], sib)
                sends.start(tok.at[s], tok.at[s], trecv.at[s], sib, nst, root)
        for k in range(4):
            b5 = fb(1 - yh, k, c)
            arrived(wb.at[b5], wrecv.at[b5], sib)
        for k in (1, 3, 2):
            for yh2 in range(2):
                b6 = fb(yh2, lax.rem(x + k, 4), 1 - c)
                arrived(wb.at[b6], wrecv.at[b6], sib)
        w_local.wait()
        t_local.wait()

    @pl.when(leaf)
    def _():
        for s in range(8):
            arrived(tok.at[s], trecv.at[s], sib)
        for yh2 in range(2):
            for k in range(4):
                b7 = fb(yh2, k, c)
                arrived(wb.at[b7], wrecv.at[b7], sib)
            for k in (1, 3, 2):
                b8 = fb(yh2, lax.rem(x + k, 4), 1 - c)
                arrived(wb.at[b8], wrecv.at[b8], sib)

    @pl.loop(0, 4)
    def _(i):
        rows = tok[pl.ds(2 * i, 2)].reshape(256, D)
        res = jnp.dot(rows, wb[...].reshape(D, 3 * COLS), preferred_element_type=F32)
        qkv[pl.ds(2 * i, 2)] = res.astype(BF16).reshape(2, 2, 64, 3 * COLS)

    @pl.loop(0, 2)
    def _(i):
        def load(at):
            return qkv[:, pl.ds(i, 1), :, at : at + HEAD].reshape(512, HEAD)

        def store(at, val):
            att[c, :, pl.ds(i, 1), :, at : at + HEAD] = val.reshape(8, 1, 64, HEAD)

        heads_of(qkv, att, load, store, None)

    sends.start(att.at[c], att.at[c], misc.at[1], sib, att.at[0])
    arrived(att.at[1 - c], misc.at[1], sib)
    arrived(pb.at[1 - yl], misc.at[0], sib)

    for n, k in enumerate((2, 1, 3, 0)):
        zt = lax.rem(z + k, 4)
        val = jnp.zeros((256, HALF), F32)
        for core in range(2):
            val += jnp.dot(
                att[core, pl.ds(2 * zt, 2)].reshape(256, COLS), pb[core], preferred_element_type=F32
            )
        val = val.astype(BF16).reshape(2, 2, 64, HALF)
        if k == 0:
            rs[z] = val
        else:
            psend[n] = val
            sends.start(
                psend.at[n], rs.at[z], rrecv.at[z], device(x, yh, yl, zt, c), psend.at[n]
            )
    for k in (1, 3, 2):
        zt = lax.rem(z + k, 4)
        arrived(rs.at[zt], rrecv.at[zt], sib)
    for y2 in range(2):
        for i in range(2):
            tot = rs[0, y2, i].astype(F32) + rs[1, y2, i].astype(F32)
            tot += rs[2, y2, i].astype(F32)
            tot += rs[3, y2, i].astype(F32)
            fin[c, y2, i] = tot.astype(BF16)

    whole_half = fin.at[0]

    @pl.when(leaf)
    def _():
        sends.start(fin.at[c], fin.at[c], misc.at[2], sib, whole_half, leaf)
        arrived(hb, misc.at[3], sib)

    @pl.when(root)
    def _():
        arrived(fin.at[1 - c], misc.at[2], sib)
        sends.start(fin.at[:, 1 - yl], hb, misc.at[3], pair, hb, root)
        hb[...] = fin[:, pl.ds(yl, 1)].reshape(2, 2, 64, HALF)

    for i in range(2):
        for r in range(0, 64, 32):
            out = jnp.concatenate([hb[0, i, r : r + 32], hb[1, i, r : r + 32]], axis=-1)
            val = x_ref[i, r : r + 32].astype(F32) + gate_ref[0:1] * out.astype(F32)
            val = val.astype(BF16)
            after_ref[i, r : r + 32] = val
            next_ref[i, r : r + 32] = normed(val.astype(F32), mod_ref[2:3], mod_ref[3:4])
    sends.finish(sib)


def temporal_kernel(
    next_ref, res_ref, w_ref, proj_ref, gate_ref,
    out_ref,
    tok, wb, pb, qkv, att, psend, rs, fin, hb,
    send_sem, trecv, rrecv, misc, local_sem,
):
    f, p, x, yh, z, yl, c = place()
    sib = device(x, yh, yl, z, 1 - c)
    far = device(x, 1 - yh, yl, z, c)
    xs = [device(lax.rem(x + k, 4), yh, yl, z, c) for k in (1, 3, 2)]
    sends = Sends(send_sem)

    def fb(y_hi, x_at, core):
        return (y_hi * 4 + x_at) * 2 + core

    barrier = pltpu.get_barrier_semaphore()
    for to in [sib, far] + xs:
        pl.semaphore_signal(barrier, inc=1, device_id=to, device_id_type=MESH)
    w_copy = pltpu.make_async_copy(w_ref, wb, local_sem.at[0])
    p_copy = pltpu.make_async_copy(proj_ref, pb, local_sem.at[1])
    w_copy.start()
    p_copy.start()
    mine = next_ref.at[:, pl.ds(pl.multiple_of(yh * 32, 32), 32)]
    other = next_ref.at[:, pl.ds(pl.multiple_of((1 - yh) * 32, 32), 32)]
    t_local = pltpu.make_async_copy(mine, tok.at[f], local_sem.at[2])
    t_local.start()
    pl.semaphore_wait(barrier, 5)
    sends.start(other, tok.at[f], trecv.at[f], far, tok.at[0])
    for to in xs:
        sends.start(mine, tok.at[f], trecv.at[f], to, tok.at[0])
    sends.start(mine, tok.at[f], trecv.at[f], sib, tok.at[0])
    g = fb(1 - yh, x, c)
    arrived(tok.at[g], trecv.at[g], sib)
    for to in xs + [sib]:
        sends.start(tok.at[g], tok.at[g], trecv.at[g], to, tok.at[0])
    for yh2 in (yh, 1 - yh):
        for k in (1, 3, 2):
            g2 = fb(yh2, lax.rem(x + k, 4), c)
            arrived(tok.at[g2], trecv.at[g2], sib)
            sends.start(tok.at[g2], tok.at[g2], trecv.at[g2], sib, tok.at[0])
    for yh2 in range(2):
        for k in range(4):
            g3 = fb(yh2, k, 1 - c)
            arrived(tok.at[g3], trecv.at[g3], sib)
    t_local.wait()
    w_copy.wait()

    @pl.loop(0, 4)
    def _(i):
        rows = tok[pl.ds(4 * i, 4)].reshape(256, D)
        res = jnp.dot(rows, wb[...], preferred_element_type=F32)
        qkv[pl.ds(4 * i, 4)] = res.astype(BF16).reshape(4, 2, 32, 3 * COLS)

    @pl.loop(0, 2)
    def _(i):
        at0 = pl.multiple_of(i * 16, 16)
        same = (
            lax.broadcasted_iota(jnp.int32, (512, 512), 0)
            - lax.broadcasted_iota(jnp.int32, (512, 512), 1)
        ) & 15 == 0

        def load(at):
            return qkv[:, :, pl.ds(at0, 16), at : at + HEAD].reshape(512, HEAD)

        def store(at, val):
            att[c, :, :, pl.ds(at0, 16), at : at + HEAD] = val.reshape(16, 2, 16, HEAD)

        heads_of(qkv, att, load, store, same)

    sends.start(att.at[c], att.at[c], misc.at[0], sib, att.at[0])
    arrived(att.at[1 - c], misc.at[0], sib)
    p_copy.wait()

    for n, k in enumerate((2, 1, 3, 0)):
        xt = lax.rem(x + k, 4)
        val = jnp.zeros((256, HALF), F32)
        for core in range(2):
            rows = jnp.concatenate(
                [
                    att[core, pl.ds(fb(yh2, xt, 0), 2)].reshape(128, COLS)
                    for yh2 in range(2)
                ],
                axis=0,
            )
            val += jnp.dot(
                rows, pb[core * COLS : (core + 1) * COLS], preferred_element_type=F32
            )
        val = val.astype(BF16).reshape(2, 2, 2, 32, HALF)
        if k == 0:
            rs[x] = val
        else:
            psend[n] = val
            sends.start(psend.at[n], rs.at[x], rrecv.at[x], device(xt, yh, yl, z, c), psend.at[n])
    for k in (1, 3, 2):
        xt = lax.rem(x + k, 4)
        arrived(rs.at[xt], rrecv.at[xt], sib)
    for core in range(2):
        for yh2 in range(2):
            tot = rs[0, yh2, core].astype(F32) + rs[1, yh2, core].astype(F32)
            tot += rs[2, yh2, core].astype(F32)
            tot += rs[3, yh2, core].astype(F32)
            fin[c, core, yh2] = tot.astype(BF16)
    sends.start(fin.at[c, 1 - c], fin.at[c, 1 - c], misc.at[1], sib, fin.at[0, 0])
    arrived(fin.at[1 - c, c], misc.at[1], sib)
    sends.start(fin.at[:, c, 1 - yh], hb, misc.at[2], far, hb)

    def finish(half, tiles):
        at = pl.ds(pl.multiple_of(half * 32, 32), 32)
        for i in range(2):
            out = jnp.concatenate([tiles[0][i], tiles[1][i]], axis=-1)
            val = res_ref[i, at].astype(F32) + gate_ref[1:2] * out.astype(F32)
            out_ref[i, at] = val.astype(BF16)

    finish(yh, [fin[n, c, yh] for n in range(2)])
    arrived(hb, misc.at[2], sib)
    finish(1 - yh, [hb[n] for n in range(2)])
    sends.finish(sib)


VMEM = pl.BlockSpec(memory_space=pltpu.VMEM)
ANY = pl.BlockSpec(memory_space=pl.ANY)


def spatial(tokens, wq, wk, wv, proj, modulation, gates):
    block = jax.ShapeDtypeStruct((2, 64, D), BF16)
    return pl.pallas_call(
        spatial_kernel,
        out_shape=(block, block),
        in_specs=[VMEM, VMEM, VMEM, VMEM, ANY, VMEM, VMEM],
        out_specs=(VMEM, VMEM),
        scratch_shapes=[
            pltpu.VMEM((2, 64, D), BF16),
            pltpu.VMEM((192, 3 * COLS), BF16),
            pltpu.VMEM((8, 2, 64, D), BF16),
            pltpu.VMEM((16, 192, 3 * COLS), BF16),
            pltpu.VMEM((2, COLS, HALF), BF16),
            pltpu.VMEM((8, 2, 64, 3 * COLS), BF16),
            pltpu.VMEM((2, 8, 2, 64, COLS), BF16),
            pltpu.VMEM((3, 2, 2, 64, HALF), BF16),
            pltpu.VMEM((4, 2, 2, 64, HALF), BF16),
            pltpu.VMEM((2, 2, 2, 64, HALF), BF16),
            pltpu.VMEM((2, 2, 64, HALF), BF16),
            pltpu.SemaphoreType.DMA((64,)),
            pltpu.SemaphoreType.DMA((8,)),
            pltpu.SemaphoreType.DMA((16,)),
            pltpu.SemaphoreType.DMA((4,)),
            pltpu.SemaphoreType.DMA((4,)),
            pltpu.SemaphoreType.DMA((3,)),
        ],
        compiler_params=pltpu.CompilerParams(
            collective_id=1, has_side_effects=True, vmem_limit_bytes=58 << 20
        ),
        cost_estimate=pl.CostEstimate(
            flops=12 * 10**9, bytes_accessed=400 << 20, transcendentals=1 << 21
        ),
        name="spatial",
    )(tokens, wq, wk, wv, proj, modulation, gates)


def temporal(normed_next, after, weights, proj, gates):
    return pl.pallas_call(
        temporal_kernel,
        out_shape=jax.ShapeDtypeStruct((2, 64, D), BF16),
        in_specs=[VMEM, VMEM, ANY, ANY, VMEM],
        out_specs=VMEM,
        scratch_shapes=[
            pltpu.VMEM((16, 2, 32, D), BF16),
            pltpu.VMEM((D, 3 * COLS), BF16),
            pltpu.VMEM((2 * COLS, HALF), BF16),
            pltpu.VMEM((16, 2, 32, 3 * COLS), BF16),
            pltpu.VMEM((2, 16, 2, 32, COLS), BF16),
            pltpu.VMEM((3, 2, 2, 2, 32, HALF), BF16),
            pltpu.VMEM((4, 2, 2, 2, 32, HALF), BF16),
            pltpu.VMEM((2, 2, 2, 2, 32, HALF), BF16),
            pltpu.VMEM((2, 2, 32, HALF), BF16),
            pltpu.SemaphoreType.DMA((24,)),
            pltpu.SemaphoreType.DMA((16,)),
            pltpu.SemaphoreType.DMA((4,)),
            pltpu.SemaphoreType.DMA((3,)),
            pltpu.SemaphoreType.DMA((3,)),
        ],
        compiler_params=pltpu.CompilerParams(
            collective_id=2, has_side_effects=True, vmem_limit_bytes=58 << 20
        ),
        cost_estimate=pl.CostEstimate(
            flops=12 * 10**9, bytes_accessed=400 << 20, transcendentals=1 << 21
        ),
        name="temporal",
    )(normed_next, after, weights, proj, gates)


def temporal_weights(wq, wk, wv, proj):
    axes = ("frame", "patch")
    joined = jnp.concatenate([wq, wk, wv], axis=1)
    pieces = []
    for parity in range(2):
        perm = []
        for f in range(16):
            for p in range(8):
                pick = (parity + f // 8) % 2
                perm.append(((2 * p + pick) * 8 + f % 8, f * 8 + p))
        pieces.append(lax.ppermute(joined, axes, perm))
    swap = lax.axis_index("frame") >= 8
    first = jnp.where(swap, pieces[1], pieces[0])
    second = jnp.where(swap, pieces[0], pieces[1])
    weights = lax.all_gather(
        jnp.concatenate([first, second], axis=0), "patch", axis=0, tiled=True
    )
    f = lax.axis_index("frame")
    x, core = lax.rem(lax.div(f, 2), 4), lax.rem(f, 2)
    part = lax.dynamic_slice(proj, (x * 96, core * HALF), (96, HALF))
    perm = []
    for y_hi in range(2):
        for xs in range(4):
            for c in range(2):
                for block in range(8):
                    src = ((y_hi * 4 + xs) * 2 + c) * 8 + block
                    dst = ((y_hi * 4 + block // 2) * 2 + c) * 8 + (block % 2) * 4 + xs
                    perm.append((src, dst))
    part = lax.ppermute(part, axes, perm)
    proj_rows = lax.all_gather(part, "patch", axis=0, tiled=True)
    return weights, proj_rows


def local(
    video_tokens,
    spatial_query,
    spatial_key,
    spatial_value,
    spatial_proj,
    temporal_query,
    temporal_key,
    temporal_value,
    temporal_proj,
    modulation,
    branch_gates,
):
    weights, proj_rows = temporal_weights(
        temporal_query, temporal_key, temporal_value, temporal_proj
    )
    after_spatial, normed_next = spatial(
        video_tokens,
        spatial_query,
        spatial_key,
        spatial_value,
        spatial_proj,
        modulation,
        branch_gates,
    )
    after_temporal = temporal(normed_next, after_spatial, weights, proj_rows, branch_gates)
    return (after_spatial, after_temporal)


def solution(mesh):
    placed = (
        P("frame", "patch", None),
        P("frame", "patch"),
        P("frame", "patch"),
        P("frame", "patch"),
        P("patch", None),
        P("frame", "patch"),
        P("frame", "patch"),
        P("frame", "patch"),
        P("patch", None),
        P(),
        P(),
    )
    return jax.shard_map(
        local,
        mesh=mesh,
        in_specs=placed,
        out_specs=(P("frame", "patch", None), P("frame", "patch", None)),
        check_vma=False,
    )
```

```python
import functools

import jax
import jax.numpy as jnp
from jax import lax
from jax.experimental import pallas as pl
from jax.experimental.pallas import tpu as pltpu
from jax.sharding import PartitionSpec as P

D = 3072
HEAD = 128
COLS = 384
PACK = 3 * COLS
HALF = D // 2
EPS = 1e-06
MESH = pl.DeviceIdType.MESH
BF16 = jnp.bfloat16
F32 = jnp.float32


def device(x, y_hi, y_lo, z, core):
    return ((y_hi * 4 + x) * 2 + core, z * 2 + y_lo)


def remote(src, dst, send, recv, to):
    return pltpu.make_async_remote_copy(
        src_ref=src, dst_ref=dst, send_sem=send, recv_sem=recv, device_id=to, device_id_type=MESH
    )


class Sends:
    def __init__(self, sems, first):
        self.sems = sems
        self.used = first
        self.open = []

    def start(self, src, dst, recv, to, like, when=None):
        at = self.used
        self.used += 1
        self.open.append((at, like, when))
        remote(src, dst, self.sems.at[at], recv, to).start()

    def finish(self, to):
        def drain(group):
            for at, like, _ in group:
                remote(like, like, self.sems.at[at], self.sems.at[at], to).wait_send()

        conditions = []
        for _, _, when in self.open:
            if not any(when is other for other in conditions):
                conditions.append(when)
        for condition in conditions:
            group = [copy for copy in self.open if copy[2] is condition]
            if condition is None:
                drain(group)
            else:
                pl.when(condition)(functools.partial(drain, group))


def normed(values, shift, scale):
    center = values - jnp.mean(values, axis=-1, keepdims=True)
    spread = jnp.mean(center * center, axis=-1, keepdims=True)
    return (center * lax.rsqrt(spread + EPS) * (1.0 + scale) + shift).astype(BF16)


def three_heads(load, store, mask):
    for h in range(3):
        q = load(h * HEAD)
        k = load(COLS + h * HEAD)
        v = load(2 * COLS + h * HEAD)
        s = lax.dot_general(q, k, (((1,), (1,)), ((), ())), preferred_element_type=F32)
        s = s * (float(HEAD) ** -0.5)
        if mask is not None:
            s = jnp.where(mask, s, -1e30)
        e = jnp.exp(s - jnp.max(s, axis=-1, keepdims=True))
        total = jnp.sum(e, axis=-1, keepdims=True)
        o = jnp.dot(e.astype(BF16), v, preferred_element_type=F32) / total
        store(h * HEAD, o.astype(BF16))


def kernel(
    x_ref, wq, wk, wv, proj_ref, tq, tk, tv, tproj_ref, mod_ref, gate_ref,
    after_ref, out_ref, wt, pt,
    xp, wst, tst, tok, tok2, wb, pb, qkv, qkv2, att, att2,
    psend, relay, rsum, hold, own, fin, xres, aft, nxt, home, hop, xch, fin2, hb,
    send_sem, trecv, wrecv, wtrecv, ptrecv, t2recv, relay_sem, rsum_sem, misc, local_sem,
):
    f = lax.axis_index("frame")
    p = lax.axis_index("patch")
    x, yh, c = lax.rem(lax.div(f, 2), 4), lax.div(f, 8), lax.rem(f, 2)
    z, yl = lax.div(p, 2), lax.rem(p, 2)
    root = c == yl
    leaf = c != yl
    sib = device(x, yh, yl, z, 1 - c)
    pair = device(x, yh, 1 - yl, z, c)
    cross = device(x, 1 - yh, 1 - yl, z, c)
    far = device(x, 1 - yh, yl, z, c)
    at_x = [lax.rem(x + k, 4) for k in range(4)]
    at_z = [lax.rem(z + k, 4) for k in range(4)]
    xs = [device(at_x[k], yh, yl, z, c) for k in range(4)]
    zs = [device(x, yh, yl, at_z[k], c) for k in range(4)]
    ys = [pair, cross, far]
    sends = Sends(send_sem, 64)
    reused = Sends(send_sem, 0)
    w_like, t_like, b_like = wst, xp, xp.at[0]

    def arrived(dst, recv):
        remote(dst, dst, recv, recv, sib).wait_recv()

    def fb(y_hi, x_at, core):
        return (y_hi * 4 + x_at) * 2 + core

    def send_w(b, to, when):
        reused.start(wb.at[b], wb.at[b], wrecv.at[b], to, w_like, when)

    def got_w(b):
        arrived(wb.at[b], wrecv.at[b])

    def send_tok(s, to, when):
        sends.start(tok.at[s], tok.at[s], trecv.at[s], to, t_like, when)

    def got_tok(s):
        arrived(tok.at[s], trecv.at[s])

    def is_mine(g):
        return lax.div(4 - lax.rem(g - x + 4, 4), 4)

    def slot(g, a):
        here = is_mine(g)
        return here * fb(yh, x, a) + (1 - here) * (16 + 2 * g + a)

    def send_wt(src, dst, to, when):
        sends.start(wt.at[src], wt.at[dst], wtrecv.at[dst], to, w_like, when)

    def got_wt(b):
        arrived(wt.at[b], wtrecv.at[b])

    def pslot(g):
        here = is_mine(g)
        return here * (yl * 4 + x) + (1 - here) * (8 + g)

    def got_pt(b):
        arrived(pt.at[b], ptrecv.at[b])

    p_like = pt.at[0]
    barrier = pltpu.get_barrier_semaphore()
    for to in [sib] + xs[1:] + zs[1:] + ys:
        pl.semaphore_signal(barrier, inc=1, device_id=to, device_id_type=MESH)
    for n, ref in enumerate((wq, wk, wv)):
        wst[:, n * COLS : (n + 1) * COLS] = ref[...]
    for n, ref in enumerate((tq, tk, tv)):
        tst[:, n * COLS : (n + 1) * COLS] = ref[...]
    half = pl.ds(pl.multiple_of(c * HALF, HALF), HALF)
    quarter = tproj_ref.at[pl.ds(pl.multiple_of(x * 96, 32), 96), half]
    p_local = pltpu.make_async_copy(proj_ref.at[:, half], pb.at[yl], local_sem.at[0])
    p_local.start()
    pt_local = pltpu.make_async_copy(quarter, pt.at[pslot(z)], local_sem.at[1])
    pt_local.start()
    w_local = pltpu.make_async_copy(wst, wb.at[f], local_sem.at[2])
    wt_local = pltpu.make_async_copy(tst, wt.at[slot(z, c)], local_sem.at[3])
    x_local = pltpu.make_async_copy(x_ref.at[c], xres.at[yl], local_sem.at[4])
    xp_local = pltpu.make_async_copy(xp.at[c], xres.at[1 - yl], local_sem.at[5])
    pl.semaphore_wait(barrier, 10)

    @pl.when(leaf)
    def _():
        sends.start(x_ref, xp, misc.at[0], pair, t_like, leaf)
        sends.start(wst, wb.at[f], wrecv.at[f], sib, w_like, leaf)
        sends.start(tst, wt.at[slot(z, c)], wtrecv.at[slot(z, c)], sib, w_like, leaf)

    def norm_to_tok(src, s):
        @pl.loop(0, 8)
        def _(n):
            i, r = n // 4, pl.multiple_of((n % 4) * 16, 16)
            tok[s, i, pl.ds(r, 16)] = normed(
                src[i, pl.ds(r, 16)].astype(F32), mod_ref[0:1], mod_ref[1:2]
            )

    q = z * 2 + 1 - yl

    @pl.when(root)
    def _():
        w_local.start()
        wt_local.start()
        x_local.start()
        for to in xs[1:] + [pair, cross]:
            sends.start(wst, wb.at[f], wrecv.at[f], to, w_like, root)
        norm_to_tok(x_ref, p)
        for to in (zs[1], zs[3], sib):
            send_tok(p, to, root)
        sends.start(x_ref.at[1 - c], xres.at[yl], misc.at[1], sib, b_like, root)
        b = fb(yh, x, 1 - c)
        got_w(b)
        for to in ys + [xs[1], xs[3]]:
            send_w(b, to, root)
        arrived(xp, misc.at[0])
        xp_local.start()
        norm_to_tok(xp, q)
        for to in (zs[1], zs[3], sib):
            send_tok(q, to, root)
        sends.start(xp.at[1 - c], xres.at[1 - yl], misc.at[2], sib, b_like, root)
        for k in (1, 3, 2):
            b2 = fb(yh, at_x[k], c)
            got_w(b2)
            send_w(b2, pair, root)
            send_w(b2, cross, root)
        wt_local.wait()
        b3 = slot(z, 1 - c)
        got_wt(b3)
        for to in (zs[1], zs[3]):
            for a in (c, 1 - c):
                send_wt(slot(z, a), slot(z, a), to, root)
        b4 = fb(1 - yh, x, 1 - c)
        got_w(b4)
        send_w(b4, xs[1], root)
        send_w(b4, xs[3], root)

    @pl.when(leaf)
    def _():
        for yh2 in (yh, 1 - yh):
            b5 = fb(yh2, x, 1 - c)
            got_w(b5)
            send_w(b5, xs[1], leaf)
            send_w(b5, xs[3], leaf)
        for k in range(2):
            b6 = fb(yh, at_x[k], c)
            got_w(b6)
            send_w(b6, cross, leaf)
            b7 = fb(1 - yh, at_x[3 - k], c)
            got_w(b7)
            send_w(b7, pair, leaf)

    pt_local.wait()
    for k in (1, 3, 2):
        sends.start(pt.at[pslot(z)], pt.at[pslot(z)], ptrecv.at[pslot(z)], zs[k], p_like)

    @pl.when(root)
    def _():
        for y2 in (yl, 1 - yl):
            s1 = at_z[3] * 2 + y2
            got_tok(s1)
            sends.start(tok.at[s1, 0], tok.at[s1, 0], trecv.at[s1], zs[1], b_like, root)
            send_tok(s1, sib, root)
            s2 = at_z[1] * 2 + y2
            got_tok(s2)
            sends.start(tok.at[s2, 1], tok.at[s2, 1], trecv.at[s2], zs[3], b_like, root)
            send_tok(s2, sib, root)

    for yh2 in range(2):
        b8 = fb(yh2, at_x[3], 1 - c)
        got_w(b8)
        b9 = fb(yh2, at_x[1], 1 - c)
        got_w(b9)
        if yh2 == 0:
            send_w(b8, xs[1], None)
        else:
            send_w(b9, xs[3], None)

    @pl.when(root)
    def _():
        for k, a, to in ((3, 0, 1), (1, 1, 3)):
            for a2 in range(2):
                got_wt(slot(at_z[k], a2))
            send_wt(slot(at_z[k], a), slot(at_z[k], a), zs[to], root)

    p_local.wait()
    rows = (pl.ds(0, 192), pl.ds(192, 192))
    proj_like = pb.at[0, pl.ds(0, 192)]
    for n, to in enumerate((pair, cross)):
        part = pb.at[yl, rows[n]]
        reused.start(part, part, misc.at[3 + n], to, proj_like)

    for k in (1, 3, 2):
        got_pt(pslot(at_z[k]))
    for k in (1, 3, 2):
        sends.start(
            pt.at[pslot(at_x[k])], pt.at[yl * 4 + x], ptrecv.at[yl * 4 + x], xs[k], p_like
        )

    @pl.when(root)
    def _():
        for y2 in (yl, 1 - yl):
            s3 = at_z[2] * 2 + y2
            got_tok(s3)
            send_tok(s3, sib, root)
        for a in range(2):
            got_wt(slot(at_z[2], a))
        for k in (1, 3, 2):
            for a in range(2):
                send_wt(slot(at_x[k], a), fb(yh, x, a), xs[k], root)
        for k in range(4):
            got_w(fb(1 - yh, k, c))
        w_local.wait()
        x_local.wait()
        xp_local.wait()

    @pl.when(leaf)
    def _():
        for s in range(8):
            got_tok(s)
        for k in range(2):
            got_w(fb(yh, at_x[2 + k], c))
            got_w(fb(1 - yh, at_x[k], c))

    for yh2 in range(2):
        got_w(fb(yh2, at_x[2], 1 - c))

    @pl.loop(0, 4)
    def _(i):
        rows4 = tok[pl.ds(2 * i, 2)].reshape(256, D)
        res = jnp.dot(rows4, wb[...].reshape(D, PACK), preferred_element_type=F32)
        qkv[pl.ds(2 * i, 2)] = res.astype(BF16).reshape(2, 2, 64, PACK)

    @pl.loop(0, 2)
    def _(i):
        def load(at):
            return qkv[:, pl.ds(i, 1), :, at : at + HEAD].reshape(512, HEAD)

        def store(at, val):
            att[c, :, pl.ds(i, 1), :, at : at + HEAD] = val.reshape(8, 1, 64, HEAD)

        three_heads(load, store, None)

    sends.start(att.at[c], att.at[c], misc.at[5], sib, att.at[0])

    for k in (1, 3, 2):
        got_pt(yl * 4 + at_x[k])
    for n, to in enumerate((pair, cross)):
        for m in range(2):
            b10 = yl * 4 + 2 * n + m
            sends.start(pt.at[b10], pt.at[b10], ptrecv.at[b10], to, p_like)

    @pl.when(root)
    def _():
        for k in range(4):
            for a in range(2):
                if k:
                    got_wt(fb(yh, at_x[k], a))
        for k in range(4):
            for a in range(2):
                b11 = fb(yh, at_x[k], a)
                send_wt(b11, b11, pair, root)
                b12 = fb(yh, at_x[3 - k], a)
                send_wt(b12, b12, cross, root)

    arrived(att.at[1 - c], misc.at[5])
    for n in range(2):
        part = pb.at[1 - yl, rows[n]]
        arrived(part, misc.at[3 + n])

    def reduce_ring(phase, take, at, to, mats, middle):
        ps, rl, rsm = psend.at[phase], relay.at[phase], rsum.at[phase]
        rl_sem, rs_sem = relay_sem.at[phase], rsum_sem.at[phase]
        like = psend.at[phase, 0]

        def term(k):
            val = jnp.dot(take(0, at[k]), mats(0), preferred_element_type=F32)
            return val + jnp.dot(take(1, at[k]), mats(1), preferred_element_type=F32)

        def send(n, val, dst, sem, k):
            ps[n] = val.astype(BF16)
            sends.start(ps.at[n], dst, sem, to[k], like)

        val = term(2)
        send(0, val[:128], rl.at[0], rl_sem.at[0], 1)
        send(1, val[128:], rl.at[1], rl_sem.at[1], 3)
        val = term(1)
        send(2, val[128:], rsm.at[0, 1], rs_sem.at[0, 1], 1)
        hold[0] = val[:128]
        val = term(3)
        send(3, val[:128], rsm.at[1, 0], rs_sem.at[1, 0], 3)
        hold[1] = val[128:]
        own[...] = term(0)
        arrived(rl.at[0], rl_sem.at[0])
        send(4, hold[0] + rl[0].astype(F32), rsm.at[0, 0], rs_sem.at[0, 0], 1)
        arrived(rl.at[1], rl_sem.at[1])
        send(5, hold[1] + rl[1].astype(F32), rsm.at[1, 1], rs_sem.at[1, 1], 3)
        middle()
        for side in range(2):
            for n in range(2):
                arrived(rsm.at[side, n], rs_sem.at[side, n])

        def total(start, size):
            n, r = start // 128, start % 128
            val = own[start : start + size] + rsm[0, n, r : r + size].astype(F32)
            return (val + rsm[1, n, r : r + size].astype(F32)).astype(BF16)

        return total

    def forward_weights():
        @pl.when(leaf)
        def _():
            for k in range(2):
                for a in range(2):
                    b13 = fb(yh, at_x[k], a)
                    got_wt(b13)
                    send_wt(b13, b13, cross, leaf)
                    b14 = fb(1 - yh, at_x[3 - k], a)
                    got_wt(b14)
                    send_wt(b14, b14, pair, leaf)

    total = reduce_ring(
        0,
        lambda core, z2: att[core, pl.ds(2 * z2, 2)].reshape(256, COLS),
        at_z,
        zs,
        lambda core: pb[core],
        forward_weights,
    )

    for y2 in range(2):
        both = [total(y2 * 128 + i * 64, 64) for i in range(2)]
        fin[c, y2] = jnp.where(c == 0, both[0], both[1])
        xch[y2] = jnp.where(c == 0, both[1], both[0])
    sends.start(xch, fin.at[c], misc.at[6], sib, xch)

    @pl.when(leaf)
    def _():
        arrived(xres.at[0], misc.at[1])
        arrived(xres.at[0], misc.at[2])

    arrived(fin.at[1 - c], misc.at[6])

    @pl.loop(0, 8)
    def _(n):
        y2, r = n // 4, pl.multiple_of((n % 4) * 16, 16)
        out = jnp.concatenate([fin[0, y2, pl.ds(r, 16)], fin[1, y2, pl.ds(r, 16)]], axis=-1)
        val = xres[y2, pl.ds(r, 16)].astype(F32) + gate_ref[0:1] * out.astype(F32)
        val = val.astype(BF16)
        aft[y2, pl.ds(r, 16)] = val
        nxt[y2, pl.ds(r, 16)] = normed(val.astype(F32), mod_ref[2:3], mod_ref[3:4])

    n_like = nxt.at[0, pl.ds(0, 32)]

    def piece(y_hi, y_lo):
        return nxt.at[y_lo, pl.ds(pl.multiple_of(y_hi * 32, 32), 32)]

    def t2(y_hi, x_at, y_lo, i):
        return tok2.at[y_hi, x_at, y_lo, i], t2recv.at[fb(y_hi, x_at, y_lo) * 2 + i]

    mine, mine_sem = t2(yh, x, yl, c)
    t2_local = pltpu.make_async_copy(piece(yh, yl), mine, local_sem.at[6])
    t2_local.start()
    for y2, l2, to in ((1 - yh, yl, far), (yh, 1 - yl, pair), (1 - yh, 1 - yl, cross)):
        sends.start(piece(y2, l2), mine, mine_sem, to, n_like)
    for to in (xs[1], xs[3], sib):
        sends.start(piece(yh, yl), mine, mine_sem, to, n_like)
    lines = ((yh, yl), (yh, 1 - yl), (1 - yh, 1 - yl), (1 - yh, yl))
    for y2, l2 in lines[1:]:
        dst, sem = t2(y2, x, l2, c)
        arrived(dst, sem)
        for to in (xs[1], xs[3], sib):
            sends.start(dst, dst, sem, to, n_like)

    a_like = aft.at[0]
    home_local = pltpu.make_async_copy(aft.at[yl], home.at[c], local_sem.at[7])

    @pl.when(leaf)
    def _():
        sends.start(aft.at[1 - yl], hop, misc.at[7], sib, a_like, leaf)
        sends.start(aft.at[yl], home.at[c], misc.at[8], sib, a_like, leaf)

    @pl.when(root)
    def _():
        home_local.start()

    for n, (y2, l2) in enumerate(lines):
        for k, to in ((3, 1), (1, 3)):
            dst, sem = t2(y2, at_x[k], l2, c)
            arrived(dst, sem)
            if (n < 2) == (k == 3):
                sends.start(dst, dst, sem, xs[to], n_like)
            sends.start(dst, dst, sem, sib, n_like)

    @pl.when(root)
    def _():
        sends.start(aft.at[1 - yl], home.at[c], misc.at[9], pair, a_like, root)
        arrived(hop, misc.at[7])
        sends.start(hop, home.at[1 - c], misc.at[10], pair, a_like, root)

    @pl.when(root)
    def _():
        for k in range(4):
            for a in range(2):
                got_wt(fb(1 - yh, at_x[k], a))

    @pl.when(leaf)
    def _():
        for k in range(2):
            for a in range(2):
                got_wt(fb(yh, at_x[2 + k], a))
                got_wt(fb(1 - yh, at_x[k], a))

    for m in range(4):
        got_pt((1 - yl) * 4 + m)
    reused.finish(sib)
    w2_local = pltpu.make_async_copy(wt.at[pl.ds(0, 16)], wb, local_sem.at[8])
    w2_local.start()
    p2_local = [
        pltpu.make_async_copy(
            pt.at[m], pb.at[m // 4, pl.ds(96 * (m % 4), 96)], local_sem.at[9 + m]
        )
        for m in range(8)
    ]
    for copy in p2_local:
        copy.start()
    t2_local.wait()
    w2_local.wait()

    for k in (0, 3, 1, 2):
        for y2, l2 in lines:
            if k == 2:
                dst, sem = t2(y2, at_x[k], l2, c)
                arrived(dst, sem)
                sends.start(dst, dst, sem, sib, n_like)
        for y2, l2 in lines:
            dst, sem = t2(y2, at_x[k], l2, 1 - c)
            arrived(dst, sem)
        rows4 = tok2[:, pl.ds(at_x[k], 1)].reshape(256, D)
        res = jnp.dot(rows4, wb[...].reshape(D, PACK), preferred_element_type=F32)
        qkv2[:, pl.ds(at_x[k], 1)] = res.astype(BF16).reshape(2, 1, 2, 2, 32, PACK)

    @pl.loop(0, 2)
    def _(i):
        at0 = pl.multiple_of(i * 16, 16)
        same = (
            lax.broadcasted_iota(jnp.int32, (512, 512), 0)
            - lax.broadcasted_iota(jnp.int32, (512, 512), 1)
        ) & 15 == 0

        def load(at):
            return qkv2[:, :, :, :, pl.ds(at0, 16), at : at + HEAD].reshape(512, HEAD)

        def store(at, val):
            att2[c, :, :, :, :, pl.ds(at0, 16), at : at + HEAD] = val.reshape(
                2, 4, 2, 2, 16, HEAD
            )

        three_heads(load, store, same)

    sends.start(att2.at[c], att2.at[c], misc.at[11], sib, att2.at[0])

    @pl.when(leaf)
    def _():
        arrived(home.at[0], misc.at[9])
        arrived(home.at[0], misc.at[10])

    @pl.when(root)
    def _():
        home_local.wait()
        arrived(home.at[0], misc.at[8])

    after_local = pltpu.make_async_copy(home, after_ref, local_sem.at[17])
    after_local.start()
    for copy in p2_local:
        copy.wait()
    arrived(att2.at[1 - c], misc.at[11])

    total = reduce_ring(
        1,
        lambda core, x2: att2[core, :, pl.ds(x2, 1)].reshape(256, COLS),
        at_x,
        xs,
        lambda core: pb[core],
        lambda: None,
    )

    for l2 in range(2):
        for y2 in range(2):
            fin2[c, l2, y2] = total(y2 * 128 + l2 * 64, 64).reshape(2, 32, HALF)
    sends.start(fin2.at[c, 1 - c], fin2.at[c, 1 - c], misc.at[12], sib, fin2.at[0, 0])
    arrived(fin2.at[1 - c, c], misc.at[12])
    sends.start(fin2.at[:, c, 1 - yh], hb, misc.at[13], far, hb)

    def finish(part, tiles):
        at = pl.ds(pl.multiple_of(part * 32, 32), 32)
        for i in range(2):
            out = jnp.concatenate([tiles[0][i], tiles[1][i]], axis=-1)
            val = home[i, at].astype(F32) + gate_ref[1:2] * out.astype(F32)
            out_ref[i, at] = val.astype(BF16)

    finish(yh, [fin2[n, c, yh] for n in range(2)])
    arrived(hb, misc.at[13])
    finish(1 - yh, [hb[n] for n in range(2)])
    after_local.wait()
    sends.finish(sib)


VMEM = pl.BlockSpec(memory_space=pltpu.VMEM)
ANY = pl.BlockSpec(memory_space=pl.ANY)
HBM = pl.BlockSpec(memory_space=pltpu.HBM)


def local(*args):
    block = jax.ShapeDtypeStruct((2, 64, D), BF16)

    def buffer(*shape, dtype=BF16):
        return pltpu.VMEM(shape, dtype)

    def sems(*shape):
        return pltpu.SemaphoreType.DMA(shape)

    outs = pl.pallas_call(
        kernel,
        out_shape=(
            block,
            block,
            jax.ShapeDtypeStruct((24, 192, PACK), BF16),
            jax.ShapeDtypeStruct((12, 96, HALF), BF16),
        ),
        in_specs=[VMEM, VMEM, VMEM, VMEM, ANY, VMEM, VMEM, VMEM, ANY, VMEM, VMEM],
        out_specs=(VMEM, VMEM, HBM, HBM),
        scratch_shapes=[
            buffer(2, 64, D),
            buffer(192, PACK),
            buffer(192, PACK),
            buffer(8, 2, 64, D),
            buffer(2, 4, 2, 2, 32, D),
            buffer(16, 192, PACK),
            buffer(2, COLS, HALF),
            buffer(8, 2, 64, PACK),
            buffer(2, 4, 2, 2, 32, PACK),
            buffer(2, 8, 2, 64, COLS),
            buffer(2, 2, 4, 2, 2, 32, COLS),
            buffer(2, 6, 128, HALF),
            buffer(2, 2, 128, HALF),
            buffer(2, 2, 2, 128, HALF),
            buffer(2, 128, HALF, dtype=F32),
            buffer(256, HALF, dtype=F32),
            buffer(2, 2, 64, HALF),
            buffer(2, 64, D),
            buffer(2, 64, D),
            buffer(2, 64, D),
            buffer(2, 64, D),
            buffer(64, D),
            buffer(2, 64, HALF),
            buffer(2, 2, 2, 2, 32, HALF),
            buffer(2, 2, 32, HALF),
            sems(256),
            sems(8),
            sems(16),
            sems(24),
            sems(12),
            sems(32),
            sems(2, 2),
            sems(2, 2, 2),
            sems(16),
            sems(18),
        ],
        compiler_params=pltpu.CompilerParams(
            collective_id=1, has_side_effects=True, vmem_limit_bytes=63 << 20
        ),
        cost_estimate=pl.CostEstimate(
            flops=24 * 10**9, bytes_accessed=200 << 20, transcendentals=1 << 22
        ),
        name="sublayers",
    )(*args)
    return outs[0], outs[1]


def solution(mesh):
    placed = (
        P("frame", "patch", None),
        P("frame", "patch"),
        P("frame", "patch"),
        P("frame", "patch"),
        P("patch", None),
        P("frame", "patch"),
        P("frame", "patch"),
        P("frame", "patch"),
        P("patch", None),
        P(),
        P(),
    )
    return jax.shard_map(
        local,
        mesh=mesh,
        in_specs=placed,
        out_specs=(P("frame", "patch", None), P("frame", "patch", None)),
        check_vma=False,
    )
```

```python
import functools

import jax
import jax.numpy as jnp
from jax import lax
from jax.experimental import pallas as pl
from jax.experimental.pallas import tpu as pltpu
from jax.sharding import PartitionSpec as P

D = 3072
HEAD = 128
COLS = 384
PACK = 3 * COLS
HALF = D // 2
EPS = 1e-06
MESH = pl.DeviceIdType.MESH
BF16 = jnp.bfloat16
F32 = jnp.float32


def device(x, y_hi, y_lo, z, core):
    return ((y_hi * 4 + x) * 2 + core, z * 2 + y_lo)


def remote(src, dst, send, recv, to):
    return pltpu.make_async_remote_copy(
        src_ref=src, dst_ref=dst, send_sem=send, recv_sem=recv, device_id=to, device_id_type=MESH
    )


class Sends:
    def __init__(self, sems, first):
        self.sems = sems
        self.used = first
        self.open = []

    def start(self, src, dst, recv, to, like, when=None):
        at = self.used
        self.used += 1
        self.open.append((at, like, when))
        remote(src, dst, self.sems.at[at], recv, to).start()

    def finish(self, to):
        def drain(group):
            for at, like, _ in group:
                remote(like, like, self.sems.at[at], self.sems.at[at], to).wait_send()

        conditions = []
        for _, _, when in self.open:
            if not any(when is other for other in conditions):
                conditions.append(when)
        for condition in conditions:
            group = [copy for copy in self.open if copy[2] is condition]
            if condition is None:
                drain(group)
            else:
                pl.when(condition)(functools.partial(drain, group))


def normed(values, shift, scale):
    center = values - jnp.mean(values, axis=-1, keepdims=True)
    spread = jnp.mean(center * center, axis=-1, keepdims=True)
    return (center * lax.rsqrt(spread + EPS) * (1.0 + scale) + shift).astype(BF16)


def three_heads(load, store, mask):
    for h in range(3):
        q = load(h * HEAD)
        k = load(COLS + h * HEAD)
        v = load(2 * COLS + h * HEAD)
        s = lax.dot_general(q, k, (((1,), (1,)), ((), ())), preferred_element_type=F32)
        s = s * (float(HEAD) ** -0.5)
        if mask is not None:
            s = jnp.where(mask, s, -1e30)
        e = jnp.exp(s - jnp.max(s, axis=-1, keepdims=True))
        total = jnp.sum(e, axis=-1, keepdims=True)
        o = jnp.dot(e.astype(BF16), v, preferred_element_type=F32) / total
        store(h * HEAD, o.astype(BF16))


def kernel(
    x_ref, wq, wk, wv, proj_ref, tq, tk, tv, tproj_ref, mod_ref, gate_ref,
    after_ref, out_ref, wt, pt,
    xp, wst, tst, tok, tok2, wb, pb, qkv, qkv2, att, att2,
    psend, relay, rsum, hold, own, fin, xres, aft, nxt, home, hop, xch, fin2, hb,
    send_sem, trecv, wrecv, wtrecv, ptrecv, t2recv, relay_sem, rsum_sem, misc, local_sem,
):
    f = lax.axis_index("frame")
    p = lax.axis_index("patch")
    x, yh, c = lax.rem(lax.div(f, 2), 4), lax.div(f, 8), lax.rem(f, 2)
    z, yl = lax.div(p, 2), lax.rem(p, 2)
    root = c == yl
    leaf = c != yl
    sib = device(x, yh, yl, z, 1 - c)
    pair = device(x, yh, 1 - yl, z, c)
    cross = device(x, 1 - yh, 1 - yl, z, c)
    far = device(x, 1 - yh, yl, z, c)
    at_x = [lax.rem(x + k, 4) for k in range(4)]
    at_z = [lax.rem(z + k, 4) for k in range(4)]
    xs = [device(at_x[k], yh, yl, z, c) for k in range(4)]
    zs = [device(x, yh, yl, at_z[k], c) for k in range(4)]
    ys = [pair, cross, far]
    sends = Sends(send_sem, 96)
    reused = Sends(send_sem, 0)
    w_like, wh_like, t_like, b_like = wst, wst.at[pl.ds(0, 96)], xp, xp.at[0]

    def arrived(dst, recv):
        remote(dst, dst, recv, recv, sib).wait_recv()

    def fb(y_hi, x_at, core):
        return (y_hi * 4 + x_at) * 2 + core

    def w_part(b, part):
        return wb.at[b] if part is None else wb.at[b, pl.ds(96 * part, 96)]

    def w_sem(b, part):
        return wrecv.at[2 * b + (part or 0)]

    def send_w(b, part, targets, when):
        ref = w_part(b, part)
        for to in targets:
            reused.start(ref, ref, w_sem(b, part), to, w_like if part is None else wh_like, when)

    def got_w(b, part):
        arrived(w_part(b, part), w_sem(b, part))

    def send_tok(s, to, when):
        sends.start(tok.at[s], tok.at[s], trecv.at[s], to, t_like, when)

    def got_tok(s):
        arrived(tok.at[s], trecv.at[s])

    def is_mine(g):
        return lax.div(4 - lax.rem(g - x + 4, 4), 4)

    def slot(g, a):
        here = is_mine(g)
        return here * fb(yh, x, a) + (1 - here) * (16 + 2 * g + a)

    def send_wt(src, dst, to, when):
        sends.start(wt.at[src], wt.at[dst], wtrecv.at[dst], to, w_like, when)

    def got_wt(b):
        arrived(wt.at[b], wtrecv.at[b])

    def pslot(g):
        here = is_mine(g)
        return here * (yl * 4 + x) + (1 - here) * (8 + g)

    def got_pt(b):
        arrived(pt.at[b], ptrecv.at[b])

    p_like = pt.at[0]
    barrier = pltpu.get_barrier_semaphore()
    for to in [sib] + xs[1:] + zs[1:] + ys:
        pl.semaphore_signal(barrier, inc=1, device_id=to, device_id_type=MESH)
    for n, ref in enumerate((wq, wk, wv)):
        wst[:, n * COLS : (n + 1) * COLS] = ref[...]
    for n, ref in enumerate((tq, tk, tv)):
        tst[:, n * COLS : (n + 1) * COLS] = ref[...]
    half = pl.ds(pl.multiple_of(c * HALF, HALF), HALF)
    quarter = tproj_ref.at[pl.ds(pl.multiple_of(x * 96, 32), 96), half]
    p_local = pltpu.make_async_copy(proj_ref.at[:, half], pb.at[yl], local_sem.at[0])
    p_local.start()
    pt_local = pltpu.make_async_copy(quarter, pt.at[pslot(z)], local_sem.at[1])
    pt_local.start()
    w_local = pltpu.make_async_copy(wst, wb.at[f], local_sem.at[2])
    wt_local = pltpu.make_async_copy(tst, wt.at[slot(z, c)], local_sem.at[3])
    x_local = pltpu.make_async_copy(x_ref.at[c], xres.at[yl], local_sem.at[4])
    xp_local = pltpu.make_async_copy(xp.at[c], xres.at[1 - yl], local_sem.at[5])
    pl.semaphore_wait(barrier, 10)

    @pl.when(leaf)
    def _():
        sends.start(x_ref, xp, misc.at[0], pair, t_like, leaf)
        sends.start(wst, wb.at[f], w_sem(f, None), sib, w_like, leaf)
        sends.start(tst, wt.at[slot(z, c)], wtrecv.at[slot(z, c)], sib, w_like, leaf)

    def norm_to_tok(src, s):
        @pl.loop(0, 8)
        def _(n):
            i, r = n // 4, pl.multiple_of((n % 4) * 16, 16)
            tok[s, i, pl.ds(r, 16)] = normed(
                src[i, pl.ds(r, 16)].astype(F32), mod_ref[0:1], mod_ref[1:2]
            )

    q = z * 2 + 1 - yl

    @pl.when(root)
    def _():
        w_local.start()
        wt_local.start()
        x_local.start()
        for part, targets in ((0, xs[1:] + [pair, cross]), (1, [xs[1], xs[3]] + ys)):
            at = pl.ds(96 * part, 96)
            for to in targets:
                sends.start(wst.at[at], wb.at[f, at], w_sem(f, part), to, wh_like, root)
        here = slot(z, c)
        for to in (zs[1], zs[3]):
            sends.start(tst, wt.at[here], wtrecv.at[here], to, w_like, root)
        norm_to_tok(x_ref, p)
        for to in (zs[1], zs[3], sib):
            send_tok(p, to, root)
        b = fb(yh, x, 1 - c)
        got_w(b, None)
        send_w(b, None, [xs[1], xs[3]] + ys, root)
        b3 = slot(z, 1 - c)
        got_wt(b3)
        for to in (zs[1], zs[3]):
            send_wt(b3, b3, to, root)
        for k in (1, 3):
            b2 = fb(yh, at_x[k], c)
            got_w(b2, 0)
            send_w(b2, 0, [pair, cross], root)
        b4 = fb(1 - yh, x, c)
        got_w(b4, 1)
        send_w(b4, 1, [xs[1], xs[3]], root)
        arrived(xp, misc.at[0])
        xp_local.start()
        norm_to_tok(xp, q)
        for to in (zs[1], zs[3], sib):
            send_tok(q, to, root)
        b2 = fb(yh, at_x[2], c)
        got_w(b2, 0)
        send_w(b2, 0, [pair, cross], root)
        b4 = fb(1 - yh, x, 1 - c)
        got_w(b4, None)
        send_w(b4, None, [xs[1], xs[3]], root)
        sends.start(x_ref.at[1 - c], xres.at[yl], misc.at[1], sib, b_like, root)
        sends.start(xp.at[1 - c], xres.at[1 - yl], misc.at[2], sib, b_like, root)

    @pl.when(leaf)
    def _():
        def pass_on(k, from_pair):
            b6 = fb(yh, at_x[k], c) if from_pair else fb(1 - yh, at_x[k], c)
            got_w(b6, 0)
            send_w(b6, 0, [cross if from_pair else pair], leaf)

        def along_x(y_hi, core, part):
            b5 = fb(y_hi, x, core)
            got_w(b5, part)
            send_w(b5, part, [xs[1], xs[3]], leaf)

        along_x(yh, c, 1)
        along_x(1 - yh, c, 1)
        pass_on(0, True)
        along_x(yh, 1 - c, None)
        along_x(1 - yh, 1 - c, None)
        pass_on(3, False)
        pass_on(1, True)
        pass_on(2, False)

    @pl.when(root)
    def _():
        for y2 in (yl, 1 - yl):
            s1 = at_z[3] * 2 + y2
            got_tok(s1)
            sends.start(tok.at[s1, 0], tok.at[s1, 0], trecv.at[s1], zs[1], b_like, root)
            send_tok(s1, sib, root)
            s2 = at_z[1] * 2 + y2
            got_tok(s2)
            sends.start(tok.at[s2, 1], tok.at[s2, 1], trecv.at[s2], zs[3], b_like, root)
            send_tok(s2, sib, root)

    for yh2 in range(2):
        for core, part in ((c, 1), (1 - c, None)):
            b8 = fb(yh2, at_x[3], core)
            got_w(b8, part)
            b9 = fb(yh2, at_x[1], core)
            got_w(b9, part)
            if yh2 == 0:
                send_w(b8, part, [xs[1]], None)
            else:
                send_w(b9, part, [xs[3]], None)

    p_local.wait()
    rows = (pl.ds(0, 192), pl.ds(192, 192))
    proj_like = pb.at[0, pl.ds(0, 192)]
    for n, to in enumerate((pair, cross)):
        part = pb.at[yl, rows[n]]
        reused.start(part, part, misc.at[3 + n], to, proj_like)

    @pl.when(root)
    def _():
        for k, a, to in ((3, 0, 1), (1, 1, 3)):
            for a2 in range(2):
                got_wt(slot(at_z[k], a2))
            send_wt(slot(at_z[k], a), slot(at_z[k], a), zs[to], root)
        for y2 in (yl, 1 - yl):
            s3 = at_z[2] * 2 + y2
            got_tok(s3)
            send_tok(s3, sib, root)

    pt_local.wait()
    for k in (1, 3, 2):
        sends.start(pt.at[pslot(z)], pt.at[pslot(z)], ptrecv.at[pslot(z)], zs[k], p_like)

    @pl.when(root)
    def _():
        for k in range(4):
            got_w(fb(1 - yh, at_x[k], c), 0)
        w_local.wait()
        x_local.wait()
        xp_local.wait()
        wt_local.wait()

    @pl.when(leaf)
    def _():
        for s in range(8):
            got_tok(s)
        for k in range(2):
            got_w(fb(yh, at_x[2 + k], c), 0)
            got_w(fb(1 - yh, at_x[k], c), 0)

    for yh2 in range(2):
        for core, part in ((c, 1), (1 - c, None)):
            got_w(fb(yh2, at_x[2], core), part)

    def along_y(k):
        for a in range(2):
            b11 = fb(yh, at_x[k], a)
            if k:
                got_wt(b11)
            send_wt(b11, b11, pair, root)
            send_wt(b11, b11, cross, root)

    def pass_along(k, from_pair):
        for a in range(2):
            b13 = fb(yh if from_pair else 1 - yh, at_x[k], a)
            got_wt(b13)
            send_wt(b13, b13, cross if from_pair else pair, leaf)

    @pl.when(root)
    def _():
        for a in range(2):
            got_wt(slot(at_z[2], a))
        for k in (1, 3, 2):
            for a in range(2):
                send_wt(slot(at_x[k], a), fb(yh, x, a), xs[k], root)
        along_y(0)

    @pl.loop(0, 4)
    def _(i):
        rows4 = tok[pl.ds(2 * i, 2)].reshape(256, D)
        res = jnp.dot(rows4, wb[...].reshape(D, PACK), preferred_element_type=F32)
        qkv[pl.ds(2 * i, 2)] = res.astype(BF16).reshape(2, 2, 64, PACK)

    @pl.loop(0, 2)
    def _(i):
        def load(at):
            return qkv[:, pl.ds(i, 1), :, at : at + HEAD].reshape(512, HEAD)

        def store(at, val):
            att[c, :, pl.ds(i, 1), :, at : at + HEAD] = val.reshape(8, 1, 64, HEAD)

        three_heads(load, store, None)

    sends.start(att.at[c], att.at[c], misc.at[5], sib, att.at[0])

    arrived(att.at[1 - c], misc.at[5])
    for n in range(2):
        part = pb.at[1 - yl, rows[n]]
        arrived(part, misc.at[3 + n])

    def reduce_ring(phase, take, at, to, mats, middle, later):
        ps, rl, rsm = psend.at[phase], relay.at[phase], rsum.at[phase]
        rl_sem, rs_sem = relay_sem.at[phase], rsum_sem.at[phase]
        like = psend.at[phase, 0]

        def term(k):
            val = jnp.dot(take(0, at[k]), mats(0), preferred_element_type=F32)
            return val + jnp.dot(take(1, at[k]), mats(1), preferred_element_type=F32)

        def send(n, val, dst, sem, k):
            ps[n] = val.astype(BF16)
            sends.start(ps.at[n], dst, sem, to[k], like)

        val = term(2)
        send(0, val[:128], rl.at[0], rl_sem.at[0], 1)
        send(1, val[128:], rl.at[1], rl_sem.at[1], 3)
        val = term(1)
        send(2, val[128:], rsm.at[0, 1], rs_sem.at[0, 1], 1)
        hold[0] = val[:128]
        val = term(3)
        send(3, val[:128], rsm.at[1, 0], rs_sem.at[1, 0], 3)
        hold[1] = val[128:]
        own[...] = term(0).reshape(2, 128, HALF)
        middle()
        arrived(rl.at[0], rl_sem.at[0])
        send(4, hold[0] + rl[0].astype(F32), rsm.at[0, 0], rs_sem.at[0, 0], 1)
        arrived(rl.at[1], rl_sem.at[1])
        send(5, hold[1] + rl[1].astype(F32), rsm.at[1, 1], rs_sem.at[1, 1], 3)
        later()
        for side in range(2):
            for n in range(2):
                arrived(rsm.at[side, n], rs_sem.at[side, n])

        def total(n, start):
            at = pl.ds(start, 64)
            val = own[n, at] + rsm[0, n, at].astype(F32)
            return (val + rsm[1, n, at].astype(F32)).astype(BF16)

        return total

    def some_weights():
        @pl.when(root)
        def _():
            along_y(1)
            along_y(3)

    def more_weights():
        @pl.when(root)
        def _():
            along_y(2)

        @pl.when(leaf)
        def _():
            pass_along(0, True)
            pass_along(3, False)
            pass_along(1, True)

        for k in (1, 3, 2):
            got_pt(pslot(at_z[k]))
        for k in (1, 3, 2):
            sends.start(
                pt.at[pslot(at_x[k])], pt.at[yl * 4 + x], ptrecv.at[yl * 4 + x], xs[k], p_like
            )

    total = reduce_ring(
        0,
        lambda core, z2: att[core, pl.ds(2 * z2, 2)].reshape(256, COLS),
        at_z,
        zs,
        lambda core: pb[core],
        some_weights,
        more_weights,
    )

    reused.finish(sib)

    def fill(n, y_hi, x_at, blocks):
        at = pl.ds(fb(y_hi, x_at, 0), blocks)
        return pltpu.make_async_copy(wt.at[at], wb.at[at], local_sem.at[n])

    @pl.when(root)
    def _():
        fill(18, yh, 0, 8).start()

    @pl.when(leaf)
    def _():
        for n, (y_hi, k) in enumerate(((yh, 0), (1 - yh, 3), (yh, 1))):
            fill(18 + n, y_hi, at_x[k], 2).start()

    for y2 in range(2):
        both = [total(y2, i * 64) for i in range(2)]
        fin[c, y2] = jnp.where(c == 0, both[0], both[1])
        xch[y2] = jnp.where(c == 0, both[1], both[0])
    sends.start(xch, fin.at[c], misc.at[6], sib, xch)

    @pl.when(leaf)
    def _():
        arrived(xres.at[0], misc.at[1])
        arrived(xres.at[0], misc.at[2])

    arrived(fin.at[1 - c], misc.at[6])

    @pl.loop(0, 8)
    def _(n):
        y2, r = n // 4, pl.multiple_of((n % 4) * 16, 16)
        out = jnp.concatenate([fin[0, y2, pl.ds(r, 16)], fin[1, y2, pl.ds(r, 16)]], axis=-1)
        val = xres[y2, pl.ds(r, 16)].astype(F32) + gate_ref[0:1] * out.astype(F32)
        val = val.astype(BF16)
        aft[y2, pl.ds(r, 16)] = val
        nxt[y2, pl.ds(r, 16)] = normed(val.astype(F32), mod_ref[2:3], mod_ref[3:4])

    n_like = nxt.at[0, pl.ds(0, 32)]

    def piece(y_hi, y_lo):
        return nxt.at[y_lo, pl.ds(pl.multiple_of(y_hi * 32, 32), 32)]

    def t2(y_hi, x_at, y_lo, i):
        return tok2.at[y_hi, x_at, y_lo, i], t2recv.at[fb(y_hi, x_at, y_lo) * 2 + i]

    mine, mine_sem = t2(yh, x, yl, c)
    t2_local = pltpu.make_async_copy(piece(yh, yl), mine, local_sem.at[6])
    t2_local.start()
    for y2, l2, to in ((1 - yh, yl, far), (yh, 1 - yl, pair), (1 - yh, 1 - yl, cross)):
        sends.start(piece(y2, l2), mine, mine_sem, to, n_like)
    for to in (xs[1], xs[3], sib):
        sends.start(piece(yh, yl), mine, mine_sem, to, n_like)
    lines = ((yh, yl), (yh, 1 - yl), (1 - yh, 1 - yl), (1 - yh, yl))
    for y2, l2 in lines[1:]:
        dst, sem = t2(y2, x, l2, c)
        arrived(dst, sem)
        for to in (xs[1], xs[3], sib):
            sends.start(dst, dst, sem, to, n_like)

    @pl.when(leaf)
    def _():
        pass_along(2, False)

    a_like = aft.at[0]
    home_local = pltpu.make_async_copy(aft.at[yl], home.at[c], local_sem.at[7])

    @pl.when(leaf)
    def _():
        sends.start(aft.at[1 - yl], hop, misc.at[7], sib, a_like, leaf)
        sends.start(aft.at[yl], home.at[c], misc.at[8], sib, a_like, leaf)

    @pl.when(root)
    def _():
        home_local.start()

    for n, (y2, l2) in enumerate(lines):
        for k, to in ((3, 1), (1, 3)):
            dst, sem = t2(y2, at_x[k], l2, c)
            arrived(dst, sem)
            if (n < 2) == (k == 3):
                sends.start(dst, dst, sem, xs[to], n_like)
            sends.start(dst, dst, sem, sib, n_like)

    @pl.when(root)
    def _():
        sends.start(aft.at[1 - yl], home.at[c], misc.at[9], pair, a_like, root)
        arrived(hop, misc.at[7])
        sends.start(hop, home.at[1 - c], misc.at[10], pair, a_like, root)

    for k in (1, 3, 2):
        got_pt(yl * 4 + at_x[k])
    for n, to in enumerate((pair, cross)):
        for m in range(2):
            b10 = yl * 4 + 2 * n + m
            sends.start(pt.at[b10], pt.at[b10], ptrecv.at[b10], to, p_like)

    @pl.when(root)
    def _():
        for k in range(4):
            for a in range(2):
                got_wt(fb(1 - yh, at_x[k], a))
            fill(22 + k, 1 - yh, at_x[k], 2).start()
        fill(18, yh, 0, 8).wait()
        for k in range(4):
            fill(22 + k, 1 - yh, at_x[k], 2).wait()

    @pl.when(leaf)
    def _():
        fill(21, 1 - yh, at_x[2], 2).start()
        last = ((yh, 3), (1 - yh, 1), (yh, 2), (1 - yh, 0))
        for n, (y_hi, k) in enumerate(last):
            for a in range(2):
                got_wt(fb(y_hi, at_x[k], a))
            fill(22 + n, y_hi, at_x[k], 2).start()
        for n, (y_hi, k) in enumerate(((yh, 0), (1 - yh, 3), (yh, 1), (1 - yh, 2)) + last):
            fill(18 + n, y_hi, at_x[k], 2).wait()

    t2_local.wait()

    for k in (0, 3, 1, 2):
        for y2, l2 in lines:
            if k == 2:
                dst, sem = t2(y2, at_x[k], l2, c)
                arrived(dst, sem)
                sends.start(dst, dst, sem, sib, n_like)
        for y2, l2 in lines:
            dst, sem = t2(y2, at_x[k], l2, 1 - c)
            arrived(dst, sem)
        rows4 = tok2[:, pl.ds(at_x[k], 1)].reshape(256, D)
        res = jnp.dot(rows4, wb[...].reshape(D, PACK), preferred_element_type=F32)
        qkv2[:, pl.ds(at_x[k], 1)] = res.astype(BF16).reshape(2, 1, 2, 2, 32, PACK)

    for m in range(4):
        got_pt((1 - yl) * 4 + m)
    p2_local = [
        pltpu.make_async_copy(
            pt.at[m], pb.at[m // 4, pl.ds(96 * (m % 4), 96)], local_sem.at[9 + m]
        )
        for m in range(8)
    ]
    for copy in p2_local:
        copy.start()

    @pl.loop(0, 2)
    def _(i):
        at0 = pl.multiple_of(i * 16, 16)
        same = (
            lax.broadcasted_iota(jnp.int32, (512, 512), 0)
            - lax.broadcasted_iota(jnp.int32, (512, 512), 1)
        ) & 15 == 0

        def load(at):
            return qkv2[:, :, :, :, pl.ds(at0, 16), at : at + HEAD].reshape(512, HEAD)

        def store(at, val):
            att2[c, :, :, :, :, pl.ds(at0, 16), at : at + HEAD] = val.reshape(
                2, 4, 2, 2, 16, HEAD
            )

        three_heads(load, store, same)

    sends.start(att2.at[c], att2.at[c], misc.at[11], sib, att2.at[0])

    @pl.when(leaf)
    def _():
        arrived(home.at[0], misc.at[9])
        arrived(home.at[0], misc.at[10])

    @pl.when(root)
    def _():
        home_local.wait()
        arrived(home.at[0], misc.at[8])

    after_local = pltpu.make_async_copy(home, after_ref, local_sem.at[17])
    after_local.start()
    for copy in p2_local:
        copy.wait()
    arrived(att2.at[1 - c], misc.at[11])

    total = reduce_ring(
        1,
        lambda core, x2: att2[core, :, pl.ds(x2, 1)].reshape(256, COLS),
        at_x,
        xs,
        lambda core: pb[core],
        lambda: None,
        lambda: None,
    )

    for n, y2 in enumerate((1 - yh, yh)):
        for l2 in range(2):
            fin2[y2, l2, c] = total(y2, l2 * 64).reshape(2, 32, HALF)
        part = fin2.at[y2, 1 - c, c]
        sends.start(part, part, misc.at[12 + n], sib, fin2.at[0, 0, 0])
    arrived(fin2.at[1 - yh, c, 1 - c], misc.at[12])
    sends.start(fin2.at[1 - yh, c], hb, misc.at[14], far, hb)
    arrived(fin2.at[yh, c, 1 - c], misc.at[13])

    def finish(part, tiles):
        at = pl.ds(pl.multiple_of(part * 32, 32), 32)
        for i in range(2):
            out = jnp.concatenate([tiles[0][i], tiles[1][i]], axis=-1)
            val = home[i, at].astype(F32) + gate_ref[1:2] * out.astype(F32)
            out_ref[i, at] = val.astype(BF16)

    finish(yh, [fin2[yh, c, n] for n in range(2)])
    arrived(hb, misc.at[14])
    finish(1 - yh, [hb[n] for n in range(2)])
    after_local.wait()
    sends.finish(sib)


VMEM = pl.BlockSpec(memory_space=pltpu.VMEM)
ANY = pl.BlockSpec(memory_space=pl.ANY)
HBM = pl.BlockSpec(memory_space=pltpu.HBM)


def local(*args):
    block = jax.ShapeDtypeStruct((2, 64, D), BF16)

    def buffer(*shape, dtype=BF16):
        return pltpu.VMEM(shape, dtype)

    def sems(*shape):
        return pltpu.SemaphoreType.DMA(shape)

    outs = pl.pallas_call(
        kernel,
        out_shape=(
            block,
            block,
            jax.ShapeDtypeStruct((24, 192, PACK), BF16),
            jax.ShapeDtypeStruct((12, 96, HALF), BF16),
        ),
        in_specs=[VMEM, VMEM, VMEM, VMEM, ANY, VMEM, VMEM, VMEM, ANY, VMEM, VMEM],
        out_specs=(VMEM, VMEM, HBM, HBM),
        scratch_shapes=[
            buffer(2, 64, D),
            buffer(192, PACK),
            buffer(192, PACK),
            buffer(8, 2, 64, D),
            buffer(2, 4, 2, 2, 32, D),
            buffer(16, 192, PACK),
            buffer(2, COLS, HALF),
            buffer(8, 2, 64, PACK),
            buffer(2, 4, 2, 2, 32, PACK),
            buffer(2, 8, 2, 64, COLS),
            buffer(2, 2, 4, 2, 2, 32, COLS),
            buffer(2, 6, 128, HALF),
            buffer(2, 2, 128, HALF),
            buffer(2, 2, 2, 128, HALF),
            buffer(2, 128, HALF, dtype=F32),
            buffer(2, 128, HALF, dtype=F32),
            buffer(2, 2, 64, HALF),
            buffer(2, 64, D),
            buffer(2, 64, D),
            buffer(2, 64, D),
            buffer(2, 64, D),
            buffer(64, D),
            buffer(2, 64, HALF),
            buffer(2, 2, 2, 2, 32, HALF),
            buffer(2, 2, 32, HALF),
            sems(288),
            sems(8),
            sems(32),
            sems(24),
            sems(12),
            sems(32),
            sems(2, 2),
            sems(2, 2, 2),
            sems(16),
            sems(26),
        ],
        compiler_params=pltpu.CompilerParams(
            collective_id=1, has_side_effects=True, vmem_limit_bytes=63 << 20
        ),
        cost_estimate=pl.CostEstimate(
            flops=24 * 10**9, bytes_accessed=200 << 20, transcendentals=1 << 22
        ),
        name="sublayers",
    )(*args)
    return outs[0], outs[1]


def solution(mesh):
    placed = (
        P("frame", "patch", None),
        P("frame", "patch"),
        P("frame", "patch"),
        P("frame", "patch"),
        P("patch", None),
        P("frame", "patch"),
        P("frame", "patch"),
        P("frame", "patch"),
        P("patch", None),
        P(),
        P(),
    )
    return jax.shard_map(
        local,
        mesh=mesh,
        in_specs=placed,
        out_specs=(P("frame", "patch", None), P("frame", "patch", None)),
        check_vma=False,
    )
```

```python
import functools

import jax
import jax.numpy as jnp
from jax import lax
from jax.experimental import pallas as pl
from jax.experimental.pallas import tpu as pltpu
from jax.sharding import PartitionSpec as P

D = 3072
HEAD = 128
COLS = 384
PACK = 3 * COLS
HALF = D // 2
EPS = 1e-06
MESH = pl.DeviceIdType.MESH
BF16 = jnp.bfloat16
F32 = jnp.float32


def device(x, y_hi, y_lo, z, core):
    return ((y_hi * 4 + x) * 2 + core, z * 2 + y_lo)


def remote(src, dst, send, recv, to):
    return pltpu.make_async_remote_copy(
        src_ref=src, dst_ref=dst, send_sem=send, recv_sem=recv, device_id=to, device_id_type=MESH
    )


class Sends:
    def __init__(self, sems, first):
        self.sems = sems
        self.used = first
        self.open = []

    def start(self, src, dst, recv, to, like, when=None):
        at = self.used
        self.used += 1
        self.open.append((at, like, when))
        remote(src, dst, self.sems.at[at], recv, to).start()

    def finish(self, to):
        def drain(group):
            for at, like, _ in group:
                remote(like, like, self.sems.at[at], self.sems.at[at], to).wait_send()

        conditions = []
        for _, _, when in self.open:
            if not any(when is other for other in conditions):
                conditions.append(when)
        for condition in conditions:
            group = [copy for copy in self.open if copy[2] is condition]
            if condition is None:
                drain(group)
            else:
                pl.when(condition)(functools.partial(drain, group))


def normed(values, shift, scale):
    center = values - jnp.mean(values, axis=-1, keepdims=True)
    spread = jnp.mean(center * center, axis=-1, keepdims=True)
    return (center * lax.rsqrt(spread + EPS) * (1.0 + scale) + shift).astype(BF16)


def three_heads(load, store, mask):
    for h in range(3):
        q = load(h * HEAD)
        k = load(COLS + h * HEAD)
        v = load(2 * COLS + h * HEAD)
        s = lax.dot_general(q, k, (((1,), (1,)), ((), ())), preferred_element_type=F32)
        s = s * (float(HEAD) ** -0.5)
        if mask is not None:
            s = jnp.where(mask, s, -1e30)
        e = jnp.exp(s - jnp.max(s, axis=-1, keepdims=True))
        total = jnp.sum(e, axis=-1, keepdims=True)
        o = jnp.dot(e.astype(BF16), v, preferred_element_type=F32) / total
        store(h * HEAD, o.astype(BF16))


def kernel(
    x_ref, wq, wk, wv, proj_ref, tq, tk, tv, tproj_ref, mod_ref, gate_ref,
    after_ref, out_ref, wt, pt,
    xp, wst, tst, tok, tok2, wb, pb, qkv, qkv2, att, att2,
    psend, relay, rsum, hold, own, fin, xres, aft, nxt, home, hop, xch, fin2, hb,
    send_sem, trecv, wrecv, wtrecv, ptrecv, t2recv, relay_sem, rsum_sem, misc, local_sem,
):
    f = lax.axis_index("frame")
    p = lax.axis_index("patch")
    x, yh, c = lax.rem(lax.div(f, 2), 4), lax.div(f, 8), lax.rem(f, 2)
    z, yl = lax.div(p, 2), lax.rem(p, 2)
    root = c == yl
    leaf = c != yl
    sib = device(x, yh, yl, z, 1 - c)
    pair = device(x, yh, 1 - yl, z, c)
    cross = device(x, 1 - yh, 1 - yl, z, c)
    far = device(x, 1 - yh, yl, z, c)
    at_x = [lax.rem(x + k, 4) for k in range(4)]
    at_z = [lax.rem(z + k, 4) for k in range(4)]
    xs = [device(at_x[k], yh, yl, z, c) for k in range(4)]
    zs = [device(x, yh, yl, at_z[k], c) for k in range(4)]
    ys = [pair, cross, far]
    sends = Sends(send_sem, 96)
    reused = Sends(send_sem, 0)
    w_like, wh_like, t_like, b_like = wst, wst.at[pl.ds(0, 96)], xp, xp.at[0]

    def arrived(dst, recv):
        remote(dst, dst, recv, recv, sib).wait_recv()

    def fb(y_hi, x_at, core):
        return (y_hi * 4 + x_at) * 2 + core

    def w_part(b, part):
        return wb.at[b] if part is None else wb.at[b, pl.ds(96 * part, 96)]

    def w_sem(b, part):
        return wrecv.at[2 * b + (part or 0)]

    def send_w(b, part, targets, when):
        ref = w_part(b, part)
        for to in targets:
            reused.start(ref, ref, w_sem(b, part), to, w_like if part is None else wh_like, when)

    def got_w(b, part):
        arrived(w_part(b, part), w_sem(b, part))

    def send_tok(s, to, when):
        sends.start(tok.at[s], tok.at[s], trecv.at[s], to, t_like, when)

    def got_tok(s):
        arrived(tok.at[s], trecv.at[s])

    def is_mine(g):
        return lax.div(4 - lax.rem(g - x + 4, 4), 4)

    def slot(g, a):
        here = is_mine(g)
        return here * fb(yh, x, a) + (1 - here) * (16 + 2 * g + a)

    def send_wt(src, dst, to, when):
        sends.start(wt.at[src], wt.at[dst], wtrecv.at[dst], to, w_like, when)

    def got_wt(b):
        arrived(wt.at[b], wtrecv.at[b])

    def pslot(g):
        here = is_mine(g)
        return here * (yl * 4 + x) + (1 - here) * (8 + g)

    def got_pt(b):
        arrived(pt.at[b], ptrecv.at[b])

    p_like = pt.at[0]
    barrier = pltpu.get_barrier_semaphore()
    for to in [sib] + xs[1:] + zs[1:] + ys:
        pl.semaphore_signal(barrier, inc=1, device_id=to, device_id_type=MESH)
    for n, ref in enumerate((wq, wk, wv)):
        wst[:, n * COLS : (n + 1) * COLS] = ref[...]
    for n, ref in enumerate((tq, tk, tv)):
        tst[:, n * COLS : (n + 1) * COLS] = ref[...]
    half = pl.ds(pl.multiple_of(c * HALF, HALF), HALF)
    quarter = tproj_ref.at[pl.ds(pl.multiple_of(x * 96, 32), 96), half]
    p_local = pltpu.make_async_copy(proj_ref.at[:, half], pb.at[yl], local_sem.at[0])
    p_local.start()
    pt_local = pltpu.make_async_copy(quarter, pt.at[pslot(z)], local_sem.at[1])
    pt_local.start()
    w_local = pltpu.make_async_copy(wst, wb.at[f], local_sem.at[2])
    wt_local = pltpu.make_async_copy(tst, wt.at[slot(z, c)], local_sem.at[3])
    x_local = pltpu.make_async_copy(x_ref.at[c], xres.at[yl], local_sem.at[4])
    xp_local = pltpu.make_async_copy(xp.at[c], xres.at[1 - yl], local_sem.at[5])
    pl.semaphore_wait(barrier, 10)

    @pl.when(leaf)
    def _():
        sends.start(x_ref, xp, misc.at[0], pair, t_like, leaf)
        sends.start(wst, wb.at[f], w_sem(f, None), sib, w_like, leaf)
        sends.start(tst, wt.at[slot(z, c)], wtrecv.at[slot(z, c)], sib, w_like, leaf)

    def norm_to_tok(src, s):
        @pl.loop(0, 8)
        def _(n):
            i, r = n // 4, pl.multiple_of((n % 4) * 16, 16)
            tok[s, i, pl.ds(r, 16)] = normed(
                src[i, pl.ds(r, 16)].astype(F32), mod_ref[0:1], mod_ref[1:2]
            )

    q = z * 2 + 1 - yl

    @pl.when(root)
    def _():
        w_local.start()
        wt_local.start()
        x_local.start()
        for part, targets in ((0, xs[1:] + [pair, cross]), (1, [xs[1], xs[3]] + ys)):
            at = pl.ds(96 * part, 96)
            for to in targets:
                sends.start(wst.at[at], wb.at[f, at], w_sem(f, part), to, wh_like, root)
        here = slot(z, c)
        for to in (zs[1], zs[3]):
            sends.start(tst, wt.at[here], wtrecv.at[here], to, w_like, root)
        norm_to_tok(x_ref, p)
        for to in (zs[1], zs[3], sib):
            send_tok(p, to, root)
        b = fb(yh, x, 1 - c)
        got_w(b, None)
        send_w(b, None, [xs[1], xs[3]] + ys, root)
        b3 = slot(z, 1 - c)
        got_wt(b3)
        for to in (zs[1], zs[3]):
            send_wt(b3, b3, to, root)
        for k in (1, 3):
            b2 = fb(yh, at_x[k], c)
            got_w(b2, 0)
            send_w(b2, 0, [pair, cross], root)
        b4 = fb(1 - yh, x, c)
        got_w(b4, 1)
        send_w(b4, 1, [xs[1], xs[3]], root)
        arrived(xp, misc.at[0])
        xp_local.start()
        norm_to_tok(xp, q)
        for to in (zs[1], zs[3], sib):
            send_tok(q, to, root)
        b2 = fb(yh, at_x[2], c)
        got_w(b2, 0)
        send_w(b2, 0, [pair, cross], root)
        b4 = fb(1 - yh, x, 1 - c)
        got_w(b4, None)
        send_w(b4, None, [xs[1], xs[3]], root)
        sends.start(x_ref.at[1 - c], xres.at[yl], misc.at[1], sib, b_like, root)
        sends.start(xp.at[1 - c], xres.at[1 - yl], misc.at[2], sib, b_like, root)

    @pl.when(leaf)
    def _():
        def pass_on(k, from_pair):
            b6 = fb(yh, at_x[k], c) if from_pair else fb(1 - yh, at_x[k], c)
            got_w(b6, 0)
            send_w(b6, 0, [cross if from_pair else pair], leaf)

        def along_x(y_hi, core, part):
            b5 = fb(y_hi, x, core)
            got_w(b5, part)
            send_w(b5, part, [xs[1], xs[3]], leaf)

        along_x(yh, c, 1)
        along_x(1 - yh, c, 1)
        pass_on(0, True)
        along_x(yh, 1 - c, None)
        along_x(1 - yh, 1 - c, None)
        pass_on(3, False)
        pass_on(1, True)
        pass_on(2, False)

    @pl.when(root)
    def _():
        for y2 in (yl, 1 - yl):
            s1 = at_z[3] * 2 + y2
            got_tok(s1)
            sends.start(tok.at[s1, 0], tok.at[s1, 0], trecv.at[s1], zs[1], b_like, root)
            send_tok(s1, sib, root)
            s2 = at_z[1] * 2 + y2
            got_tok(s2)
            sends.start(tok.at[s2, 1], tok.at[s2, 1], trecv.at[s2], zs[3], b_like, root)
            send_tok(s2, sib, root)

    for yh2 in range(2):
        for core, part in ((c, 1), (1 - c, None)):
            b8 = fb(yh2, at_x[3], core)
            got_w(b8, part)
            b9 = fb(yh2, at_x[1], core)
            got_w(b9, part)
            if yh2 == 0:
                send_w(b8, part, [xs[1]], None)
            else:
                send_w(b9, part, [xs[3]], None)

    p_local.wait()
    rows = (pl.ds(0, 192), pl.ds(192, 192))
    proj_like = pb.at[0, pl.ds(0, 192)]
    for n, to in enumerate((pair, cross)):
        part = pb.at[yl, rows[n]]
        reused.start(part, part, misc.at[3 + n], to, proj_like)

    @pl.when(root)
    def _():
        for k, a, to in ((3, 0, 1), (1, 1, 3)):
            for a2 in range(2):
                got_wt(slot(at_z[k], a2))
            send_wt(slot(at_z[k], a), slot(at_z[k], a), zs[to], root)
        for y2 in (yl, 1 - yl):
            s3 = at_z[2] * 2 + y2
            got_tok(s3)
            send_tok(s3, sib, root)

    pt_local.wait()
    for k in (1, 3, 2):
        sends.start(pt.at[pslot(z)], pt.at[pslot(z)], ptrecv.at[pslot(z)], zs[k], p_like)

    @pl.when(root)
    def _():
        for k in range(4):
            got_w(fb(1 - yh, at_x[k], c), 0)
        w_local.wait()
        x_local.wait()
        xp_local.wait()
        wt_local.wait()

    @pl.when(leaf)
    def _():
        for s in range(8):
            got_tok(s)
        for k in range(2):
            got_w(fb(yh, at_x[2 + k], c), 0)
            got_w(fb(1 - yh, at_x[k], c), 0)

    for yh2 in range(2):
        for core, part in ((c, 1), (1 - c, None)):
            got_w(fb(yh2, at_x[2], core), part)

    def to_x(k):
        for a in range(2):
            send_wt(slot(at_x[k], a), fb(yh, x, a), xs[k], root)

    def along_y(k):
        for a in range(2):
            b11 = fb(yh, at_x[k], a)
            if k:
                got_wt(b11)
            send_wt(b11, b11, pair, root)
            send_wt(b11, b11, cross, root)

    def pass_along(k, from_pair):
        for a in range(2):
            b13 = fb(yh if from_pair else 1 - yh, at_x[k], a)
            got_wt(b13)
            send_wt(b13, b13, cross if from_pair else pair, leaf)

    @pl.when(root)
    def _():
        for a in range(2):
            got_wt(slot(at_z[2], a))
        to_x(1)
        to_x(3)
        along_y(0)

    @pl.loop(0, 4)
    def _(i):
        rows4 = tok[pl.ds(2 * i, 2)].reshape(256, D)
        res = jnp.dot(rows4, wb[...].reshape(D, PACK), preferred_element_type=F32)
        qkv[pl.ds(2 * i, 2)] = res.astype(BF16).reshape(2, 2, 64, PACK)

    class Ring:
        def __init__(self, phase, take, at, to):
            self.phase, self.take, self.at, self.to = phase, take, at, to
            self.like = psend.at[phase, 0, 0]

        def term(self, stage, k):
            val = jnp.dot(self.take(stage, 0, self.at[k]), pb[0], preferred_element_type=F32)
            return val + jnp.dot(self.take(stage, 1, self.at[k]), pb[1], preferred_element_type=F32)

        def send(self, stage, n, val, dst, sem, k):
            src = psend.at[self.phase, stage, n]
            src[...] = val.astype(BF16)
            sends.start(src, dst, sem, self.to[k], self.like)

        def relay(self, stage, n):
            return relay.at[self.phase, stage, n], relay_sem.at[self.phase, stage, n]

        def last(self, stage, side, n):
            return rsum.at[self.phase, stage, side, n], rsum_sem.at[self.phase, stage, side, n]

        def begin(self, stage):
            val = self.term(stage, 2)
            self.send(stage, 0, val[:64], *self.relay(stage, 0), 1)
            self.send(stage, 1, val[64:], *self.relay(stage, 1), 3)
            val = self.term(stage, 1)
            self.send(stage, 2, val[64:], *self.last(stage, 0, 1), 1)
            hold[stage, 0] = val[:64]
            val = self.term(stage, 3)
            self.send(stage, 3, val[:64], *self.last(stage, 1, 0), 3)
            hold[stage, 1] = val[64:]
            own[stage] = self.term(stage, 0).reshape(2, 64, HALF)

        def pass_on(self, stage):
            for n, to in ((0, 1), (1, 3)):
                ref, sem = self.relay(stage, n)
                arrived(ref, sem)
                val = hold[stage, n] + ref[...].astype(F32)
                self.send(stage, 4 + n, val, *self.last(stage, n, n), to)

        def end(self, stage):
            for side in range(2):
                for n in range(2):
                    arrived(*self.last(stage, side, n))

        def total(self, stage, n):
            val = own[stage, n] + rsum[self.phase, stage, 0, n].astype(F32)
            return (val + rsum[self.phase, stage, 1, n].astype(F32)).astype(BF16)

    def spatial_heads(i):
        def load(at):
            return qkv[:, i, :, at : at + HEAD].reshape(512, HEAD)

        def store(at, val):
            att[c, i, :, :, at : at + HEAD] = val.reshape(8, 64, HEAD)

        three_heads(load, store, None)
        sends.start(att.at[c, i], att.at[c, i], misc.at[(5, 15)[i]], sib, att.at[0, 0])

    def spatial_heads_there(i):
        arrived(att.at[1 - c, i], misc.at[(5, 15)[i]])

    ring = Ring(
        0,
        lambda stage, core, z2: att[core, stage, pl.ds(2 * z2, 2)].reshape(128, COLS),
        at_z,
        zs,
    )
    spatial_heads(0)

    @pl.when(root)
    def _():
        along_y(1)
        along_y(3)
        to_x(2)

    @pl.when(leaf)
    def _():
        pass_along(0, True)

    for n in range(2):
        part = pb.at[1 - yl, rows[n]]
        arrived(part, misc.at[3 + n])
    spatial_heads_there(0)
    ring.begin(0)
    spatial_heads(1)
    ring.pass_on(0)
    spatial_heads_there(1)
    ring.begin(1)

    @pl.when(root)
    def _():
        along_y(2)

    @pl.when(leaf)
    def _():
        pass_along(3, False)

    ring.pass_on(1)

    @pl.when(leaf)
    def _():
        pass_along(1, True)

    for k in (1, 3, 2):
        got_pt(pslot(at_z[k]))
    for k in (1, 3, 2):
        sends.start(
            pt.at[pslot(at_x[k])], pt.at[yl * 4 + x], ptrecv.at[yl * 4 + x], xs[k], p_like
        )
    ring.end(0)
    ring.end(1)

    reused.finish(sib)

    def fill(n, y_hi, x_at, blocks):
        at = pl.ds(fb(y_hi, x_at, 0), blocks)
        return pltpu.make_async_copy(wt.at[at], wb.at[at], local_sem.at[n])

    @pl.when(root)
    def _():
        fill(18, yh, 0, 8).start()

    @pl.when(leaf)
    def _():
        for n, (y_hi, k) in enumerate(((yh, 0), (1 - yh, 3), (yh, 1))):
            fill(18 + n, y_hi, at_x[k], 2).start()

    for y2 in range(2):
        both = [ring.total(i, y2) for i in range(2)]
        fin[c, y2] = jnp.where(c == 0, both[0], both[1])
        xch[y2] = jnp.where(c == 0, both[1], both[0])
    sends.start(xch, fin.at[c], misc.at[6], sib, xch)

    @pl.when(leaf)
    def _():
        arrived(xres.at[0], misc.at[1])
        arrived(xres.at[0], misc.at[2])

    arrived(fin.at[1 - c], misc.at[6])

    @pl.loop(0, 8)
    def _(n):
        y2, r = n // 4, pl.multiple_of((n % 4) * 16, 16)
        out = jnp.concatenate([fin[0, y2, pl.ds(r, 16)], fin[1, y2, pl.ds(r, 16)]], axis=-1)
        aft[y2, pl.ds(r, 16)] = out
        val = xres[y2, pl.ds(r, 16)].astype(F32) + gate_ref[0:1] * out.astype(F32)
        val = val.astype(BF16)
        nxt[y2, pl.ds(r, 16)] = normed(val.astype(F32), mod_ref[2:3], mod_ref[3:4])

    n_like = nxt.at[0, pl.ds(0, 32)]

    def piece(y_hi, y_lo):
        return nxt.at[y_lo, pl.ds(pl.multiple_of(y_hi * 32, 32), 32)]

    def t2(y_hi, x_at, y_lo, i):
        return tok2.at[y_hi, x_at, y_lo, i], t2recv.at[fb(y_hi, x_at, y_lo) * 2 + i]

    mine, mine_sem = t2(yh, x, yl, c)
    t2_local = pltpu.make_async_copy(piece(yh, yl), mine, local_sem.at[6])
    t2_local.start()
    for y2, l2, to in ((1 - yh, yl, far), (yh, 1 - yl, pair), (1 - yh, 1 - yl, cross)):
        sends.start(piece(y2, l2), mine, mine_sem, to, n_like)
    for to in (xs[1], xs[3], sib):
        sends.start(piece(yh, yl), mine, mine_sem, to, n_like)
    lines = ((yh, yl), (yh, 1 - yl), (1 - yh, 1 - yl), (1 - yh, yl))

    @pl.when(leaf)
    def _():
        pass_along(2, False)

    for y2, l2 in lines[1:]:
        dst, sem = t2(y2, x, l2, c)
        arrived(dst, sem)
        for to in (xs[1], xs[3], sib):
            sends.start(dst, dst, sem, to, n_like)

    a_like = aft.at[0]
    home_local = pltpu.make_async_copy(aft.at[yl], home.at[c], local_sem.at[7])

    @pl.when(leaf)
    def _():
        sends.start(aft.at[1 - yl], hop, misc.at[7], sib, a_like, leaf)
        sends.start(aft.at[yl], home.at[c], misc.at[8], sib, a_like, leaf)

    @pl.when(root)
    def _():
        home_local.start()

    for n, (y2, l2) in enumerate(lines):
        for k, to in ((3, 1), (1, 3)):
            dst, sem = t2(y2, at_x[k], l2, c)
            arrived(dst, sem)
            if (n < 2) == (k == 3):
                sends.start(dst, dst, sem, xs[to], n_like)
            sends.start(dst, dst, sem, sib, n_like)

    @pl.when(root)
    def _():
        sends.start(aft.at[1 - yl], home.at[c], misc.at[9], pair, a_like, root)
        arrived(hop, misc.at[7])
        sends.start(hop, home.at[1 - c], misc.at[10], pair, a_like, root)

    for k in (1, 3, 2):
        got_pt(yl * 4 + at_x[k])
    for n, to in enumerate((pair, cross)):
        for m in range(2):
            b10 = yl * 4 + 2 * n + m
            sends.start(pt.at[b10], pt.at[b10], ptrecv.at[b10], to, p_like)

    @pl.when(root)
    def _():
        for k in range(4):
            for a in range(2):
                got_wt(fb(1 - yh, at_x[k], a))
            fill(22 + k, 1 - yh, at_x[k], 2).start()
        fill(18, yh, 0, 8).wait()
        for k in range(4):
            fill(22 + k, 1 - yh, at_x[k], 2).wait()

    @pl.when(leaf)
    def _():
        fill(21, 1 - yh, at_x[2], 2).start()
        last = ((yh, 3), (1 - yh, 1), (yh, 2), (1 - yh, 0))
        for n, (y_hi, k) in enumerate(last):
            for a in range(2):
                got_wt(fb(y_hi, at_x[k], a))
            fill(22 + n, y_hi, at_x[k], 2).start()
        for n, (y_hi, k) in enumerate(((yh, 0), (1 - yh, 3), (yh, 1), (1 - yh, 2)) + last):
            fill(18 + n, y_hi, at_x[k], 2).wait()

    t2_local.wait()

    for k in (0, 3, 1, 2):
        for y2, l2 in lines:
            if k == 2:
                dst, sem = t2(y2, at_x[k], l2, c)
                arrived(dst, sem)
                sends.start(dst, dst, sem, sib, n_like)
        for y2, l2 in lines:
            dst, sem = t2(y2, at_x[k], l2, 1 - c)
            arrived(dst, sem)
        rows4 = tok2[:, pl.ds(at_x[k], 1)].reshape(256, D)
        res = jnp.dot(rows4, wb[...].reshape(D, PACK), preferred_element_type=F32)
        qkv2[:, pl.ds(at_x[k], 1)] = res.astype(BF16).reshape(2, 1, 2, 2, 32, PACK)

    for m in range(4):
        got_pt((1 - yl) * 4 + m)
    p2_local = [
        pltpu.make_async_copy(
            pt.at[m], pb.at[m // 4, pl.ds(96 * (m % 4), 96)], local_sem.at[9 + m]
        )
        for m in range(8)
    ]
    for copy in p2_local:
        copy.start()

    @pl.loop(0, 2)
    def _(i):
        at0 = pl.multiple_of(i * 16, 16)
        same = (
            lax.broadcasted_iota(jnp.int32, (512, 512), 0)
            - lax.broadcasted_iota(jnp.int32, (512, 512), 1)
        ) & 15 == 0

        def load(at):
            return qkv2[:, :, :, :, pl.ds(at0, 16), at : at + HEAD].reshape(512, HEAD)

        def store(at, val):
            att2[c, :, :, :, :, pl.ds(at0, 16), at : at + HEAD] = val.reshape(
                2, 4, 2, 2, 16, HEAD
            )

        three_heads(load, store, same)

    sends.start(att2.at[c], att2.at[c], misc.at[11], sib, att2.at[0])

    @pl.when(leaf)
    def _():
        arrived(home.at[0], misc.at[9])
        arrived(home.at[0], misc.at[10])

    @pl.when(root)
    def _():
        home_local.wait()
        arrived(home.at[0], misc.at[8])

    after_local = pltpu.make_async_copy(home, after_ref, local_sem.at[17])
    after_local.start()
    for copy in p2_local:
        copy.wait()
    arrived(att2.at[1 - c], misc.at[11])

    ring = Ring(
        1,
        lambda stage, core, x2: att2[core, yh if stage else 1 - yh, x2].reshape(128, COLS),
        at_x,
        xs,
    )
    ring.begin(0)
    ring.pass_on(0)
    ring.begin(1)
    ring.pass_on(1)

    def collect(stage, y2):
        ring.end(stage)
        for l2 in range(2):
            fin2[y2, l2, c] = ring.total(stage, l2).reshape(2, 32, HALF)
        part = fin2.at[y2, 1 - c, c]
        sends.start(part, part, misc.at[12 + stage], sib, fin2.at[0, 0, 0])

    collect(0, 1 - yh)
    arrived(fin2.at[1 - yh, c, 1 - c], misc.at[12])
    sends.start(fin2.at[1 - yh, c], hb, misc.at[14], far, hb)
    collect(1, yh)
    arrived(fin2.at[yh, c, 1 - c], misc.at[13])

    def finish(part, tiles):
        at = pl.ds(pl.multiple_of(part * 32, 32), 32)
        for i in range(2):
            out_ref[i, at] = jnp.concatenate([tiles[0][i], tiles[1][i]], axis=-1)

    finish(yh, [fin2[yh, c, n] for n in range(2)])
    arrived(hb, misc.at[14])
    finish(1 - yh, [hb[n] for n in range(2)])
    after_local.wait()
    sends.finish(sib)


VMEM = pl.BlockSpec(memory_space=pltpu.VMEM)
ANY = pl.BlockSpec(memory_space=pl.ANY)
HBM = pl.BlockSpec(memory_space=pltpu.HBM)


def local(*args):
    block = jax.ShapeDtypeStruct((2, 64, D), BF16)

    def buffer(*shape, dtype=BF16):
        return pltpu.VMEM(shape, dtype)

    def sems(*shape):
        return pltpu.SemaphoreType.DMA(shape)

    outs = pl.pallas_call(
        kernel,
        out_shape=(
            block,
            block,
            jax.ShapeDtypeStruct((24, 192, PACK), BF16),
            jax.ShapeDtypeStruct((12, 96, HALF), BF16),
        ),
        in_specs=[VMEM, VMEM, VMEM, VMEM, ANY, VMEM, VMEM, VMEM, ANY, VMEM, VMEM],
        out_specs=(VMEM, VMEM, HBM, HBM),
        scratch_shapes=[
            buffer(2, 64, D),
            buffer(192, PACK),
            buffer(192, PACK),
            buffer(8, 2, 64, D),
            buffer(2, 4, 2, 2, 32, D),
            buffer(16, 192, PACK),
            buffer(2, COLS, HALF),
            buffer(8, 2, 64, PACK),
            buffer(2, 4, 2, 2, 32, PACK),
            buffer(2, 2, 8, 64, COLS),
            buffer(2, 2, 4, 2, 2, 32, COLS),
            buffer(2, 2, 6, 64, HALF),
            buffer(2, 2, 2, 64, HALF),
            buffer(2, 2, 2, 2, 64, HALF),
            buffer(2, 2, 64, HALF, dtype=F32),
            buffer(2, 2, 64, HALF, dtype=F32),
            buffer(2, 2, 64, HALF),
            buffer(2, 64, D),
            buffer(2, 64, D),
            buffer(2, 64, D),
            buffer(2, 64, D),
            buffer(64, D),
            buffer(2, 64, HALF),
            buffer(2, 2, 2, 2, 32, HALF),
            buffer(2, 2, 32, HALF),
            sems(288),
            sems(8),
            sems(32),
            sems(24),
            sems(12),
            sems(32),
            sems(2, 2, 2),
            sems(2, 2, 2, 2),
            sems(16),
            sems(26),
        ],
        compiler_params=pltpu.CompilerParams(
            collective_id=1, has_side_effects=True, vmem_limit_bytes=63 << 20
        ),
        cost_estimate=pl.CostEstimate(
            flops=24 * 10**9, bytes_accessed=200 << 20, transcendentals=1 << 22
        ),
        name="sublayers",
    )(*args)
    tokens, gates = args[0].astype(F32), args[10]
    after_spatial = (tokens + gates[0] * outs[0].astype(F32)).astype(BF16)
    after_temporal = (after_spatial.astype(F32) + gates[1] * outs[1].astype(F32)).astype(BF16)
    return after_spatial, after_temporal


def solution(mesh):
    placed = (
        P("frame", "patch", None),
        P("frame", "patch"),
        P("frame", "patch"),
        P("frame", "patch"),
        P("patch", None),
        P("frame", "patch"),
        P("frame", "patch"),
        P("frame", "patch"),
        P("patch", None),
        P(),
        P(),
    )
    return jax.shard_map(
        local,
        mesh=mesh,
        in_specs=placed,
        out_specs=(P("frame", "patch", None), P("frame", "patch", None)),
        check_vma=False,
    )
```

```python
import functools

import jax
import jax.numpy as jnp
from jax import lax
from jax.experimental import pallas as pl
from jax.experimental.pallas import tpu as pltpu
from jax.sharding import PartitionSpec as P

D = 3072
HEAD = 128
COLS = 384
PACK = 3 * COLS
HALF = D // 2
EPS = 1e-06
PARTS = (pl.ds(0, 128), pl.ds(128, 64))
MESH = pl.DeviceIdType.MESH
BF16 = jnp.bfloat16
F32 = jnp.float32


def device(x, y_hi, y_lo, z, core):
    return ((y_hi * 4 + x) * 2 + core, z * 2 + y_lo)


def remote(src, dst, send, recv, to):
    return pltpu.make_async_remote_copy(
        src_ref=src, dst_ref=dst, send_sem=send, recv_sem=recv, device_id=to, device_id_type=MESH
    )


class Sends:
    def __init__(self, sems, first):
        self.sems = sems
        self.used = first
        self.open = []

    def start(self, src, dst, recv, to, like, when=None):
        at = self.used
        self.used += 1
        self.open.append((at, like, when))
        remote(src, dst, self.sems.at[at], recv, to).start()

    def finish(self, to):
        def drain(group):
            for at, like, _ in group:
                remote(like, like, self.sems.at[at], self.sems.at[at], to).wait_send()

        conditions = []
        for _, _, when in self.open:
            if not any(when is other for other in conditions):
                conditions.append(when)
        for condition in conditions:
            group = [copy for copy in self.open if copy[2] is condition]
            if condition is None:
                drain(group)
            else:
                pl.when(condition)(functools.partial(drain, group))


def normed(values, shift, scale):
    center = values - jnp.mean(values, axis=-1, keepdims=True)
    spread = jnp.mean(center * center, axis=-1, keepdims=True)
    return (center * lax.rsqrt(spread + EPS) * (1.0 + scale) + shift).astype(BF16)


def three_heads(load, store, mask):
    for h in range(3):
        q = load(h * HEAD)
        k = load(COLS + h * HEAD)
        v = load(2 * COLS + h * HEAD)
        s = lax.dot_general(q, k, (((1,), (1,)), ((), ())), preferred_element_type=F32)
        s = s * (float(HEAD) ** -0.5)
        if mask is not None:
            s = jnp.where(mask, s, -1e30)
        e = jnp.exp(s - jnp.max(s, axis=-1, keepdims=True))
        total = jnp.sum(e, axis=-1, keepdims=True)
        o = jnp.dot(e.astype(BF16), v, preferred_element_type=F32) / total
        store(h * HEAD, o.astype(BF16))


def kernel(
    x_ref, wq, wk, wv, proj_ref, tq, tk, tv, tproj_ref, mod_ref, gate_ref,
    after_ref, out_ref, wt, pt,
    xp, wst, tst, tok, tok2, wb, pb, qkv, qkv2, att, att2,
    psend, relay, rsum, hold, own, fin, xres, aft, nxt, home, hop, xch, fin2, hb,
    send_sem, trecv, wrecv, wtrecv, ptrecv, t2recv, relay_sem, rsum_sem, misc, local_sem,
):
    f = lax.axis_index("frame")
    p = lax.axis_index("patch")
    x, yh, c = lax.rem(lax.div(f, 2), 4), lax.div(f, 8), lax.rem(f, 2)
    z, yl = lax.div(p, 2), lax.rem(p, 2)
    root = c == yl
    leaf = c != yl
    sib = device(x, yh, yl, z, 1 - c)
    pair = device(x, yh, 1 - yl, z, c)
    cross = device(x, 1 - yh, 1 - yl, z, c)
    far = device(x, 1 - yh, yl, z, c)
    at_x = [lax.rem(x + k, 4) for k in range(4)]
    at_z = [lax.rem(z + k, 4) for k in range(4)]
    xs = [device(at_x[k], yh, yl, z, c) for k in range(4)]
    zs = [device(x, yh, yl, at_z[k], c) for k in range(4)]
    ys = [pair, cross, far]
    sends = Sends(send_sem, 96)
    reused = Sends(send_sem, 0)
    w_like, t_like, b_like = wst, xp, xp.at[0]
    w_likes = {None: wst, 0: wst.at[PARTS[0]], 1: wst.at[PARTS[1]]}

    def arrived(dst, recv):
        remote(dst, dst, recv, recv, sib).wait_recv()

    def fb(y_hi, x_at, core):
        return (y_hi * 4 + x_at) * 2 + core

    def w_part(b, part):
        return wb.at[b] if part is None else wb.at[b, PARTS[part]]

    def w_sem(b, part):
        return wrecv.at[2 * b + (part or 0)]

    def send_w(b, part, targets, when):
        ref = w_part(b, part)
        for to in targets:
            reused.start(ref, ref, w_sem(b, part), to, w_likes[part], when)

    def got_w(b, part):
        arrived(w_part(b, part), w_sem(b, part))

    def send_tok(s, to, when):
        sends.start(tok.at[s], tok.at[s], trecv.at[s], to, t_like, when)

    def got_tok(s):
        arrived(tok.at[s], trecv.at[s])

    def is_mine(g):
        return lax.div(4 - lax.rem(g - x + 4, 4), 4)

    def slot(g, a):
        here = is_mine(g)
        return here * fb(yh, x, a) + (1 - here) * (16 + 2 * g + a)

    def send_wt(src, dst, to, when):
        sends.start(wt.at[src], wt.at[dst], wtrecv.at[dst], to, w_like, when)

    def got_wt(b):
        arrived(wt.at[b], wtrecv.at[b])

    def pslot(g):
        here = is_mine(g)
        return here * (yl * 4 + x) + (1 - here) * (8 + g)

    def got_pt(b):
        arrived(pt.at[b], ptrecv.at[b])

    p_like = pt.at[0]
    barrier = pltpu.get_barrier_semaphore()
    for to in [sib] + xs[1:] + zs[1:] + ys:
        pl.semaphore_signal(barrier, inc=1, device_id=to, device_id_type=MESH)
    for n, ref in enumerate((wq, wk, wv)):
        wst[:, n * COLS : (n + 1) * COLS] = ref[...]
    for n, ref in enumerate((tq, tk, tv)):
        tst[:, n * COLS : (n + 1) * COLS] = ref[...]
    half = pl.ds(pl.multiple_of(c * HALF, HALF), HALF)
    quarter = tproj_ref.at[pl.ds(pl.multiple_of(x * 96, 32), 96), half]
    p_local = pltpu.make_async_copy(proj_ref.at[:, half], pb.at[yl], local_sem.at[0])
    p_local.start()
    pt_local = pltpu.make_async_copy(quarter, pt.at[pslot(z)], local_sem.at[1])
    pt_local.start()
    w_local = pltpu.make_async_copy(wst, wb.at[f], local_sem.at[2])
    wt_local = pltpu.make_async_copy(tst, wt.at[slot(z, c)], local_sem.at[3])
    x_local = pltpu.make_async_copy(x_ref.at[c], xres.at[yl], local_sem.at[4])
    xp_local = pltpu.make_async_copy(xp.at[c], xres.at[1 - yl], local_sem.at[5])
    pl.semaphore_wait(barrier, 10)

    @pl.when(leaf)
    def _():
        sends.start(x_ref, xp, misc.at[0], pair, t_like, leaf)
        sends.start(wst, wb.at[f], w_sem(f, None), sib, w_like, leaf)
        sends.start(tst, wt.at[slot(z, c)], wtrecv.at[slot(z, c)], sib, w_like, leaf)

    def norm_to_tok(src, s):
        @pl.loop(0, 8)
        def _(n):
            i, r = n // 4, pl.multiple_of((n % 4) * 16, 16)
            tok[s, i, pl.ds(r, 16)] = normed(
                src[i, pl.ds(r, 16)].astype(F32), mod_ref[0:1], mod_ref[1:2]
            )

    q = z * 2 + 1 - yl

    @pl.when(root)
    def _():
        w_local.start()
        wt_local.start()
        x_local.start()
        for part, targets in ((0, xs[1:] + [pair, cross]), (1, [xs[1], xs[3]] + ys)):
            at = PARTS[part]
            for to in targets:
                sends.start(wst.at[at], wb.at[f, at], w_sem(f, part), to, w_likes[part], root)
        here = slot(z, c)
        for to in (zs[1], zs[3]):
            sends.start(tst, wt.at[here], wtrecv.at[here], to, w_like, root)
        norm_to_tok(x_ref, p)
        for to in (zs[1], zs[3], sib):
            send_tok(p, to, root)
        b = fb(yh, x, 1 - c)
        got_w(b, None)
        send_w(b, None, [xs[1], xs[3]] + ys, root)
        b3 = slot(z, 1 - c)
        got_wt(b3)
        for to in (zs[1], zs[3]):
            send_wt(b3, b3, to, root)
        for k in (1, 3):
            b2 = fb(yh, at_x[k], c)
            got_w(b2, 0)
            send_w(b2, 0, [pair, cross], root)
        b4 = fb(1 - yh, x, c)
        got_w(b4, 1)
        send_w(b4, 1, [xs[1], xs[3]], root)
        arrived(xp, misc.at[0])
        xp_local.start()
        norm_to_tok(xp, q)
        for to in (zs[1], zs[3], sib):
            send_tok(q, to, root)
        b2 = fb(yh, at_x[2], c)
        got_w(b2, 0)
        send_w(b2, 0, [pair, cross], root)
        b4 = fb(1 - yh, x, 1 - c)
        got_w(b4, None)
        send_w(b4, None, [xs[1], xs[3]], root)
        sends.start(x_ref.at[1 - c], xres.at[yl], misc.at[1], sib, b_like, root)
        sends.start(xp.at[1 - c], xres.at[1 - yl], misc.at[2], sib, b_like, root)

    @pl.when(leaf)
    def _():
        def pass_on(k, from_pair):
            b6 = fb(yh, at_x[k], c) if from_pair else fb(1 - yh, at_x[k], c)
            got_w(b6, 0)
            send_w(b6, 0, [cross if from_pair else pair], leaf)

        def along_x(y_hi, core, part):
            b5 = fb(y_hi, x, core)
            got_w(b5, part)
            send_w(b5, part, [xs[1], xs[3]], leaf)

        along_x(yh, c, 1)
        along_x(1 - yh, c, 1)
        pass_on(0, True)
        along_x(yh, 1 - c, None)
        along_x(1 - yh, 1 - c, None)
        pass_on(3, False)
        pass_on(1, True)
        pass_on(2, False)

    @pl.when(root)
    def _():
        for y2 in (yl, 1 - yl):
            s1 = at_z[3] * 2 + y2
            got_tok(s1)
            sends.start(tok.at[s1, 0], tok.at[s1, 0], trecv.at[s1], zs[1], b_like, root)
            send_tok(s1, sib, root)
            s2 = at_z[1] * 2 + y2
            got_tok(s2)
            sends.start(tok.at[s2, 1], tok.at[s2, 1], trecv.at[s2], zs[3], b_like, root)
            send_tok(s2, sib, root)

    for yh2 in range(2):
        for core, part in ((c, 1), (1 - c, None)):
            b8 = fb(yh2, at_x[3], core)
            got_w(b8, part)
            b9 = fb(yh2, at_x[1], core)
            got_w(b9, part)
            if yh2 == 0:
                send_w(b8, part, [xs[1]], None)
            else:
                send_w(b9, part, [xs[3]], None)

    p_local.wait()
    rows = (pl.ds(0, 192), pl.ds(192, 192))
    proj_like = pb.at[0, pl.ds(0, 192)]
    for n, to in enumerate((pair, cross)):
        part = pb.at[yl, rows[n]]
        reused.start(part, part, misc.at[3 + n], to, proj_like)

    @pl.when(root)
    def _():
        for k, a, to in ((3, 0, 1), (1, 1, 3)):
            for a2 in range(2):
                got_wt(slot(at_z[k], a2))
            send_wt(slot(at_z[k], a), slot(at_z[k], a), zs[to], root)
        for y2 in (yl, 1 - yl):
            s3 = at_z[2] * 2 + y2
            got_tok(s3)
            send_tok(s3, sib, root)

    pt_local.wait()
    for k in (1, 3, 2):
        sends.start(pt.at[pslot(z)], pt.at[pslot(z)], ptrecv.at[pslot(z)], zs[k], p_like)

    @pl.when(root)
    def _():
        for k in range(4):
            got_w(fb(1 - yh, at_x[k], c), 0)
        w_local.wait()
        x_local.wait()
        xp_local.wait()
        wt_local.wait()

    @pl.when(leaf)
    def _():
        for s in range(8):
            got_tok(s)
        for k in range(2):
            got_w(fb(yh, at_x[2 + k], c), 0)
            got_w(fb(1 - yh, at_x[k], c), 0)

    for yh2 in range(2):
        for core, part in ((c, 1), (1 - c, None)):
            got_w(fb(yh2, at_x[2], core), part)

    zp = lax.rem(z, 2)

    def to_x(k):
        for a in range(2):
            send_wt(slot(at_x[k], a), fb(yh, x, a), xs[k], root)

    def along_y(k):
        if k:
            for a in range(2):
                got_wt(fb(yh, at_x[k], a))
        b11 = fb(yh, at_x[k], zp)
        send_wt(b11, b11, pair, root)
        send_wt(b11, b11, cross, root)

    def pass_along(k, from_pair):
        b13 = fb(yh if from_pair else 1 - yh, at_x[k], zp)
        got_wt(b13)
        send_wt(b13, b13, cross if from_pair else pair, leaf)

    @pl.when(root)
    def _():
        for a in range(2):
            got_wt(slot(at_z[2], a))
        to_x(1)
        to_x(3)
        along_y(0)

    @pl.loop(0, 4)
    def _(i):
        rows4 = tok[pl.ds(2 * i, 2)].reshape(256, D)
        res = jnp.dot(rows4, wb[...].reshape(D, PACK), preferred_element_type=F32)
        qkv[pl.ds(2 * i, 2)] = res.astype(BF16).reshape(2, 2, 64, PACK)

    class Ring:
        def __init__(self, phase, take, at, to):
            self.phase, self.take, self.at, self.to = phase, take, at, to
            self.like = psend.at[phase, 0, 0]

        def term(self, stage, k):
            val = jnp.dot(self.take(stage, 0, self.at[k]), pb[0], preferred_element_type=F32)
            return val + jnp.dot(self.take(stage, 1, self.at[k]), pb[1], preferred_element_type=F32)

        def send(self, stage, n, val, dst, sem, k):
            src = psend.at[self.phase, stage, n]
            src[...] = val.astype(BF16)
            sends.start(src, dst, sem, self.to[k], self.like)

        def relay(self, stage, n):
            return relay.at[self.phase, stage, n], relay_sem.at[self.phase, stage, n]

        def last(self, stage, side, n):
            return rsum.at[self.phase, stage, side, n], rsum_sem.at[self.phase, stage, side, n]

        def begin(self, stage):
            val = self.term(stage, 2)
            self.send(stage, 0, val[:64], *self.relay(stage, 0), 1)
            self.send(stage, 1, val[64:], *self.relay(stage, 1), 3)
            val = self.term(stage, 1)
            self.send(stage, 2, val[64:], *self.last(stage, 0, 1), 1)
            hold[stage, 0] = val[:64]
            val = self.term(stage, 3)
            self.send(stage, 3, val[:64], *self.last(stage, 1, 0), 3)
            hold[stage, 1] = val[64:]
            own[stage] = self.term(stage, 0).reshape(2, 64, HALF)

        def pass_on(self, stage):
            for n, to in ((0, 1), (1, 3)):
                ref, sem = self.relay(stage, n)
                arrived(ref, sem)
                val = hold[stage, n] + ref[...].astype(F32)
                self.send(stage, 4 + n, val, *self.last(stage, n, n), to)

        def end(self, stage):
            for side in range(2):
                for n in range(2):
                    arrived(*self.last(stage, side, n))

        def total(self, stage, n):
            val = own[stage, n] + rsum[self.phase, stage, 0, n].astype(F32)
            return (val + rsum[self.phase, stage, 1, n].astype(F32)).astype(BF16)

    def spatial_heads(i):
        def load(at):
            return qkv[:, i, :, at : at + HEAD].reshape(512, HEAD)

        def store(at, val):
            att[c, i, :, :, at : at + HEAD] = val.reshape(8, 64, HEAD)

        three_heads(load, store, None)
        sends.start(att.at[c, i], att.at[c, i], misc.at[(5, 15)[i]], sib, att.at[0, 0])

    def spatial_heads_there(i):
        arrived(att.at[1 - c, i], misc.at[(5, 15)[i]])

    ring = Ring(
        0,
        lambda stage, core, z2: att[core, stage, pl.ds(2 * z2, 2)].reshape(128, COLS),
        at_z,
        zs,
    )
    spatial_heads(0)

    @pl.when(root)
    def _():
        along_y(1)
        along_y(3)
        to_x(2)

    @pl.when(leaf)
    def _():
        pass_along(0, True)

    for n in range(2):
        part = pb.at[1 - yl, rows[n]]
        arrived(part, misc.at[3 + n])
    spatial_heads_there(0)
    ring.begin(0)
    spatial_heads(1)
    ring.pass_on(0)
    spatial_heads_there(1)
    ring.begin(1)

    @pl.when(root)
    def _():
        along_y(2)

    @pl.when(leaf)
    def _():
        pass_along(3, False)

    ring.pass_on(1)

    @pl.when(leaf)
    def _():
        pass_along(1, True)

    for k in (1, 3, 2):
        got_pt(pslot(at_z[k]))
    for k in (1, 3, 2):
        sends.start(
            pt.at[pslot(at_x[k])], pt.at[yl * 4 + x], ptrecv.at[yl * 4 + x], xs[k], p_like
        )
    reused.finish(sib)

    def fill(n, b, blocks=1):
        at = pl.ds(b, blocks)
        return pltpu.make_async_copy(wt.at[at], wb.at[at], local_sem.at[18 + n])

    @pl.when(root)
    def _():
        fill(0, yh * 8, 8).start()

    n_like = nxt.at[0, pl.ds(0, 32)]

    def piece(y_hi, y_lo):
        return nxt.at[y_lo, pl.ds(pl.multiple_of(y_hi * 32, 32), 32)]

    def t2(y_hi, x_at, y_lo, i):
        return tok2.at[y_hi, x_at, y_lo, i], t2recv.at[fb(y_hi, x_at, y_lo) * 2 + i]

    mine, mine_sem = t2(yh, x, yl, c)
    t2_local = pltpu.make_async_copy(piece(yh, yl), mine, local_sem.at[6])
    lines = ((yh, yl), (yh, 1 - yl), (1 - yh, 1 - yl), (1 - yh, yl))

    def slot_of_patches(y2):
        @pl.loop(0, 4)
        def _(n):
            r = pl.multiple_of(n * 16, 16)
            out = jnp.concatenate([fin[0, y2, pl.ds(r, 16)], fin[1, y2, pl.ds(r, 16)]], axis=-1)
            aft[y2, pl.ds(r, 16)] = out
            val = xres[y2, pl.ds(r, 16)].astype(F32) + gate_ref[0:1] * out.astype(F32)
            val = val.astype(BF16).astype(F32)
            nxt[y2, pl.ds(r, 16)] = normed(val, mod_ref[2:3], mod_ref[3:4])

    def settle(i, here, there):
        ring.end(i)

        @pl.when(there)
        def _():
            for y2 in range(2):
                xch[y2] = ring.total(i, y2)
            sends.start(xch, fin.at[c], misc.at[6], sib, xch, there)

        @pl.when(here)
        def _():
            for y2 in range(2):
                fin[c, y2] = ring.total(i, y2)
            arrived(fin.at[1 - c], misc.at[6])
            slot_of_patches(1 - yl)
            sends.start(piece(yh, 1 - yl), mine, mine_sem, pair, n_like, here)
            sends.start(piece(1 - yh, 1 - yl), mine, mine_sem, cross, n_like, here)
            slot_of_patches(yl)
            for to in (xs[1], xs[3], sib):
                sends.start(piece(yh, yl), mine, mine_sem, to, n_like, here)
            sends.start(piece(1 - yh, yl), mine, mine_sem, far, n_like, here)
            t2_local.start()

    @pl.when(leaf)
    def _():
        arrived(xres.at[0], misc.at[1])
        arrived(xres.at[0], misc.at[2])

    core0, core1 = c == 0, c == 1
    settle(0, core0, core1)

    @pl.when(leaf)
    def _():
        pass_along(2, False)

    settle(1, core1, core0)

    for y2, l2 in lines[1:]:
        dst, sem = t2(y2, x, l2, c)
        arrived(dst, sem)
        for to in (xs[1], xs[3], sib):
            sends.start(dst, dst, sem, to, n_like)

    leaf_blocks = ((yh, 0), (1 - yh, 3), (yh, 1), (1 - yh, 2), (yh, 3), (1 - yh, 1), (yh, 2), (1 - yh, 0))

    @pl.when(leaf)
    def _():
        for n, (y_hi, k) in enumerate(leaf_blocks):
            b15 = fb(y_hi, at_x[k], zp)
            if n >= 4:
                got_wt(b15)
            send_wt(b15, b15, zs[1 if n % 2 == 0 else 3], leaf)
            fill(n, b15).start()

    @pl.when(root)
    def _():
        for k in range(4):
            b15 = fb(1 - yh, at_x[k], zp)
            got_wt(b15)
            send_wt(b15, b15, zs[1 if k < 2 else 3], root)
            fill(1 + k, b15).start()

    a_like = aft.at[0]
    home_local = pltpu.make_async_copy(aft.at[yl], home.at[c], local_sem.at[7])

    @pl.when(leaf)
    def _():
        sends.start(aft.at[1 - yl], hop, misc.at[7], sib, a_like, leaf)
        sends.start(aft.at[yl], home.at[c], misc.at[8], sib, a_like, leaf)

    @pl.when(root)
    def _():
        home_local.start()

    for n, (y2, l2) in enumerate(lines):
        for k, to in ((3, 1), (1, 3)):
            dst, sem = t2(y2, at_x[k], l2, c)
            arrived(dst, sem)
            if (n < 2) == (k == 3):
                sends.start(dst, dst, sem, xs[to], n_like)
            sends.start(dst, dst, sem, sib, n_like)

    @pl.when(root)
    def _():
        sends.start(aft.at[1 - yl], home.at[c], misc.at[9], pair, a_like, root)
        arrived(hop, misc.at[7])
        sends.start(hop, home.at[1 - c], misc.at[10], pair, a_like, root)

    for k in (1, 3, 2):
        got_pt(yl * 4 + at_x[k])
    for n, to in enumerate((pair, cross)):
        for m in range(2):
            b10 = yl * 4 + 2 * n + m
            sends.start(pt.at[b10], pt.at[b10], ptrecv.at[b10], to, p_like)

    @pl.when(root)
    def _():
        for k in range(4):
            b16 = fb(1 - yh, at_x[k], 1 - zp)
            got_wt(b16)
            fill(5 + k, b16).start()
        fill(0, yh * 8, 8).wait()
        for k in range(4):
            for n, a in ((1 + k, zp), (5 + k, 1 - zp)):
                fill(n, fb(1 - yh, at_x[k], a)).wait()

    @pl.when(leaf)
    def _():
        for n, (y_hi, k) in enumerate(leaf_blocks):
            b16 = fb(y_hi, at_x[k], 1 - zp)
            got_wt(b16)
            fill(8 + n, b16).start()
        for n, (y_hi, k) in enumerate(leaf_blocks):
            for m, a in ((n, zp), (8 + n, 1 - zp)):
                fill(m, fb(y_hi, at_x[k], a)).wait()

    t2_local.wait()

    for k in (0, 3, 1, 2):
        for y2, l2 in lines:
            if k == 2:
                dst, sem = t2(y2, at_x[k], l2, c)
                arrived(dst, sem)
                sends.start(dst, dst, sem, sib, n_like)
        for y2, l2 in lines:
            dst, sem = t2(y2, at_x[k], l2, 1 - c)
            arrived(dst, sem)
        rows4 = tok2[:, pl.ds(at_x[k], 1)].reshape(256, D)
        res = jnp.dot(rows4, wb[...].reshape(D, PACK), preferred_element_type=F32)
        qkv2[:, pl.ds(at_x[k], 1)] = res.astype(BF16).reshape(2, 1, 2, 2, 32, PACK)

    for m in range(4):
        got_pt((1 - yl) * 4 + m)
    p2_local = [
        pltpu.make_async_copy(
            pt.at[m], pb.at[m // 4, pl.ds(96 * (m % 4), 96)], local_sem.at[9 + m]
        )
        for m in range(8)
    ]
    for copy in p2_local:
        copy.start()

    @pl.loop(0, 2)
    def _(i):
        at0 = pl.multiple_of(i * 16, 16)
        same = (
            lax.broadcasted_iota(jnp.int32, (512, 512), 0)
            - lax.broadcasted_iota(jnp.int32, (512, 512), 1)
        ) & 15 == 0

        def load(at):
            return qkv2[:, :, :, :, pl.ds(at0, 16), at : at + HEAD].reshape(512, HEAD)

        def store(at, val):
            att2[c, :, :, :, :, pl.ds(at0, 16), at : at + HEAD] = val.reshape(
                2, 4, 2, 2, 16, HEAD
            )

        three_heads(load, store, same)

    sends.start(att2.at[c], att2.at[c], misc.at[11], sib, att2.at[0])

    @pl.when(leaf)
    def _():
        arrived(home.at[0], misc.at[9])
        arrived(home.at[0], misc.at[10])

    @pl.when(root)
    def _():
        home_local.wait()
        arrived(home.at[0], misc.at[8])

    after_local = pltpu.make_async_copy(home, after_ref, local_sem.at[17])
    after_local.start()
    for copy in p2_local:
        copy.wait()
    arrived(att2.at[1 - c], misc.at[11])

    ring = Ring(
        1,
        lambda stage, core, x2: att2[core, yh if stage else 1 - yh, x2].reshape(128, COLS),
        at_x,
        xs,
    )
    ring.begin(0)
    ring.pass_on(0)
    ring.begin(1)
    ring.pass_on(1)

    def collect(stage, y2):
        ring.end(stage)
        for l2 in range(2):
            fin2[y2, l2, c] = ring.total(stage, l2).reshape(2, 32, HALF)
        part = fin2.at[y2, 1 - c, c]
        sends.start(part, part, misc.at[12 + stage], sib, fin2.at[0, 0, 0])

    collect(0, 1 - yh)
    arrived(fin2.at[1 - yh, c, 1 - c], misc.at[12])
    sends.start(fin2.at[1 - yh, c], hb, misc.at[14], far, hb)
    collect(1, yh)
    arrived(fin2.at[yh, c, 1 - c], misc.at[13])

    def finish(part, tiles):
        at = pl.ds(pl.multiple_of(part * 32, 32), 32)
        for i in range(2):
            out_ref[i, at] = jnp.concatenate([tiles[0][i], tiles[1][i]], axis=-1)

    finish(yh, [fin2[yh, c, n] for n in range(2)])
    arrived(hb, misc.at[14])
    finish(1 - yh, [hb[n] for n in range(2)])
    after_local.wait()
    sends.finish(sib)


VMEM = pl.BlockSpec(memory_space=pltpu.VMEM)
ANY = pl.BlockSpec(memory_space=pl.ANY)
HBM = pl.BlockSpec(memory_space=pltpu.HBM)


def local(*args):
    block = jax.ShapeDtypeStruct((2, 64, D), BF16)

    def buffer(*shape, dtype=BF16):
        return pltpu.VMEM(shape, dtype)

    def sems(*shape):
        return pltpu.SemaphoreType.DMA(shape)

    outs = pl.pallas_call(
        kernel,
        out_shape=(
            block,
            block,
            jax.ShapeDtypeStruct((24, 192, PACK), BF16),
            jax.ShapeDtypeStruct((12, 96, HALF), BF16),
        ),
        in_specs=[VMEM, VMEM, VMEM, VMEM, ANY, VMEM, VMEM, VMEM, ANY, VMEM, VMEM],
        out_specs=(VMEM, VMEM, HBM, HBM),
        scratch_shapes=[
            buffer(2, 64, D),
            buffer(192, PACK),
            buffer(192, PACK),
            buffer(8, 2, 64, D),
            buffer(2, 4, 2, 2, 32, D),
            buffer(16, 192, PACK),
            buffer(2, COLS, HALF),
            buffer(8, 2, 64, PACK),
            buffer(2, 4, 2, 2, 32, PACK),
            buffer(2, 2, 8, 64, COLS),
            buffer(2, 2, 4, 2, 2, 32, COLS),
            buffer(2, 2, 6, 64, HALF),
            buffer(2, 2, 2, 64, HALF),
            buffer(2, 2, 2, 2, 64, HALF),
            buffer(2, 2, 64, HALF, dtype=F32),
            buffer(2, 2, 64, HALF, dtype=F32),
            buffer(2, 2, 64, HALF),
            buffer(2, 64, D),
            buffer(2, 64, D),
            buffer(2, 64, D),
            buffer(2, 64, D),
            buffer(64, D),
            buffer(2, 64, HALF),
            buffer(2, 2, 2, 2, 32, HALF),
            buffer(2, 2, 32, HALF),
            sems(288),
            sems(8),
            sems(32),
            sems(24),
            sems(12),
            sems(32),
            sems(2, 2, 2),
            sems(2, 2, 2, 2),
            sems(16),
            sems(34),
        ],
        compiler_params=pltpu.CompilerParams(
            collective_id=1, has_side_effects=True, vmem_limit_bytes=63 << 20
        ),
        cost_estimate=pl.CostEstimate(
            flops=24 * 10**9, bytes_accessed=200 << 20, transcendentals=1 << 22
        ),
        name="sublayers",
    )(*args)
    tokens, gates = args[0].astype(F32), args[10]
    after_spatial = (tokens + gates[0] * outs[0].astype(F32)).astype(BF16)
    after_temporal = (after_spatial.astype(F32) + gates[1] * outs[1].astype(F32)).astype(BF16)
    return after_spatial, after_temporal


def solution(mesh):
    placed = (
        P("frame", "patch", None),
        P("frame", "patch"),
        P("frame", "patch"),
        P("frame", "patch"),
        P("patch", None),
        P("frame", "patch"),
        P("frame", "patch"),
        P("frame", "patch"),
        P("patch", None),
        P(),
        P(),
    )
    return jax.shard_map(
        local,
        mesh=mesh,
        in_specs=placed,
        out_specs=(P("frame", "patch", None), P("frame", "patch", None)),
        check_vma=False,
    )
```

```python
import functools

import jax
import jax.numpy as jnp
from jax import lax
from jax.experimental import pallas as pl
from jax.experimental.pallas import tpu as pltpu
from jax.sharding import PartitionSpec as P

D = 3072
HEAD = 128
COLS = 384
PACK = 3 * COLS
HALF = D // 2
EPS = 1e-06
PARTS = (pl.ds(0, 128), pl.ds(128, 64))
MESH = pl.DeviceIdType.MESH
BF16 = jnp.bfloat16
F32 = jnp.float32


def device(x, y_hi, y_lo, z, core):
    return ((y_hi * 4 + x) * 2 + core, z * 2 + y_lo)


def remote(src, dst, send, recv, to):
    return pltpu.make_async_remote_copy(
        src_ref=src, dst_ref=dst, send_sem=send, recv_sem=recv, device_id=to, device_id_type=MESH
    )


class Sends:
    def __init__(self, sems, first):
        self.sems = sems
        self.used = first
        self.open = []

    def start(self, src, dst, recv, to, like, when=None):
        at = self.used
        self.used += 1
        self.open.append((at, like, when))
        remote(src, dst, self.sems.at[at], recv, to).start()

    def finish(self, to):
        def drain(group):
            for at, like, _ in group:
                remote(like, like, self.sems.at[at], self.sems.at[at], to).wait_send()

        conditions = []
        for _, _, when in self.open:
            if not any(when is other for other in conditions):
                conditions.append(when)
        for condition in conditions:
            group = [copy for copy in self.open if copy[2] is condition]
            if condition is None:
                drain(group)
            else:
                pl.when(condition)(functools.partial(drain, group))


def normed(values, shift, scale):
    center = values - jnp.mean(values, axis=-1, keepdims=True)
    spread = jnp.mean(center * center, axis=-1, keepdims=True)
    return (center * lax.rsqrt(spread + EPS) * (1.0 + scale) + shift).astype(BF16)


def three_heads(load, store, mask):
    for h in range(3):
        q = load(h * HEAD)
        k = load(COLS + h * HEAD)
        v = load(2 * COLS + h * HEAD)
        s = lax.dot_general(q, k, (((1,), (1,)), ((), ())), preferred_element_type=F32)
        s = s * (float(HEAD) ** -0.5)
        if mask is not None:
            s = jnp.where(mask, s, -1e30)
        e = jnp.exp(s - jnp.max(s, axis=-1, keepdims=True))
        total = jnp.sum(e, axis=-1, keepdims=True)
        o = jnp.dot(e.astype(BF16), v, preferred_element_type=F32) / total
        store(h * HEAD, o.astype(BF16))


def kernel(
    x_ref, wq, wk, wv, proj_ref, tq, tk, tv, tproj_ref, mod_ref, gate_ref,
    after_ref, out_ref, wt, pt,
    xp, wst, tst, tok, tok2, wb, pb, qkv, qkv2, att, att2,
    psend, relay, rsum, hold, own, fin, xres, aft, nxt, home, hop, xch, fin2, hb,
    send_sem, trecv, wrecv, wtrecv, ptrecv, t2recv, relay_sem, rsum_sem, misc, local_sem,
):
    f = lax.axis_index("frame")
    p = lax.axis_index("patch")
    x, yh, c = lax.rem(lax.div(f, 2), 4), lax.div(f, 8), lax.rem(f, 2)
    z, yl = lax.div(p, 2), lax.rem(p, 2)
    root = c == yl
    leaf = c != yl
    sib = device(x, yh, yl, z, 1 - c)
    pair = device(x, yh, 1 - yl, z, c)
    cross = device(x, 1 - yh, 1 - yl, z, c)
    far = device(x, 1 - yh, yl, z, c)
    at_x = [lax.rem(x + k, 4) for k in range(4)]
    at_z = [lax.rem(z + k, 4) for k in range(4)]
    xs = [device(at_x[k], yh, yl, z, c) for k in range(4)]
    zs = [device(x, yh, yl, at_z[k], c) for k in range(4)]
    ys = [pair, cross, far]
    sends = Sends(send_sem, 96)
    reused = Sends(send_sem, 0)
    w_like, t_like, b_like = wst, xp, xp.at[0]
    w_likes = {None: wst, 0: wst.at[PARTS[0]], 1: wst.at[PARTS[1]]}

    def arrived(dst, recv):
        remote(dst, dst, recv, recv, sib).wait_recv()

    def fb(y_hi, x_at, core):
        return (y_hi * 4 + x_at) * 2 + core

    def w_part(b, part):
        return wb.at[b] if part is None else wb.at[b, PARTS[part]]

    def w_sem(b, part):
        return wrecv.at[2 * b + (part or 0)]

    def send_w(b, part, targets, when):
        ref = w_part(b, part)
        for to in targets:
            reused.start(ref, ref, w_sem(b, part), to, w_likes[part], when)

    def got_w(b, part):
        arrived(w_part(b, part), w_sem(b, part))

    def send_tok(s, to, when):
        sends.start(tok.at[s], tok.at[s], trecv.at[s], to, t_like, when)

    def got_tok(s):
        arrived(tok.at[s], trecv.at[s])

    def is_mine(g):
        return lax.div(4 - lax.rem(g - x + 4, 4), 4)

    def slot(g, a):
        here = is_mine(g)
        return here * fb(yh, x, a) + (1 - here) * (16 + 2 * g + a)

    def send_wt(src, dst, to, when):
        sends.start(wt.at[src], wt.at[dst], wtrecv.at[dst], to, w_like, when)

    def got_wt(b):
        arrived(wt.at[b], wtrecv.at[b])

    def pslot(g):
        here = is_mine(g)
        return here * (yl * 4 + x) + (1 - here) * (8 + g)

    def got_pt(b):
        arrived(pt.at[b], ptrecv.at[b])

    p_like = pt.at[0]
    barrier = pltpu.get_barrier_semaphore()
    for to in [sib] + xs[1:] + zs[1:] + ys:
        pl.semaphore_signal(barrier, inc=1, device_id=to, device_id_type=MESH)
    for n, ref in enumerate((wq, wk, wv)):
        wst[:, n * COLS : (n + 1) * COLS] = ref[...]
    for n, ref in enumerate((tq, tk, tv)):
        tst[:, n * COLS : (n + 1) * COLS] = ref[...]
    half = pl.ds(pl.multiple_of(c * HALF, HALF), HALF)
    quarter = tproj_ref.at[pl.ds(pl.multiple_of(x * 96, 32), 96), half]
    p_local = pltpu.make_async_copy(proj_ref.at[:, half], pb.at[yl], local_sem.at[0])
    p_local.start()
    pt_local = pltpu.make_async_copy(quarter, pt.at[pslot(z)], local_sem.at[1])
    pt_local.start()
    w_local = pltpu.make_async_copy(wst, wb.at[f], local_sem.at[2])
    wt_local = pltpu.make_async_copy(tst, wt.at[slot(z, c)], local_sem.at[3])
    x_local = pltpu.make_async_copy(x_ref.at[c], xres.at[yl], local_sem.at[4])
    xp_local = pltpu.make_async_copy(xp.at[c], xres.at[1 - yl], local_sem.at[5])
    pl.semaphore_wait(barrier, 10)

    @pl.when(leaf)
    def _():
        sends.start(x_ref, xp, misc.at[0], pair, t_like, leaf)
        sends.start(wst, wb.at[f], w_sem(f, None), sib, w_like, leaf)
        sends.start(tst, wt.at[slot(z, c)], wtrecv.at[slot(z, c)], sib, w_like, leaf)

    def norm_to_tok(src, s):
        @pl.loop(0, 8)
        def _(n):
            i, r = n // 4, pl.multiple_of((n % 4) * 16, 16)
            tok[s, i, pl.ds(r, 16)] = normed(
                src[i, pl.ds(r, 16)].astype(F32), mod_ref[0:1], mod_ref[1:2]
            )

    q = z * 2 + 1 - yl

    @pl.when(root)
    def _():
        w_local.start()
        wt_local.start()
        x_local.start()
        for part, targets in ((0, xs[1:] + [pair, cross]), (1, [xs[1], xs[3]] + ys)):
            at = PARTS[part]
            for to in targets:
                sends.start(wst.at[at], wb.at[f, at], w_sem(f, part), to, w_likes[part], root)
        here = slot(z, c)
        for to in (zs[1], zs[3]):
            sends.start(tst, wt.at[here], wtrecv.at[here], to, w_like, root)
        norm_to_tok(x_ref, p)
        for to in (zs[1], zs[3], sib):
            send_tok(p, to, root)
        b = fb(yh, x, 1 - c)
        got_w(b, None)
        send_w(b, None, [xs[1], xs[3]] + ys, root)
        b3 = slot(z, 1 - c)
        got_wt(b3)
        for to in (zs[1], zs[3]):
            send_wt(b3, b3, to, root)
        for k in (1, 3):
            b2 = fb(yh, at_x[k], c)
            got_w(b2, 0)
            send_w(b2, 0, [pair, cross], root)
        b4 = fb(1 - yh, x, c)
        got_w(b4, 1)
        send_w(b4, 1, [xs[1], xs[3]], root)
        arrived(xp, misc.at[0])
        xp_local.start()
        norm_to_tok(xp, q)
        for to in (zs[1], zs[3], sib):
            send_tok(q, to, root)
        b2 = fb(yh, at_x[2], c)
        got_w(b2, 0)
        send_w(b2, 0, [pair, cross], root)
        b4 = fb(1 - yh, x, 1 - c)
        got_w(b4, None)
        send_w(b4, None, [xs[1], xs[3]], root)
        sends.start(x_ref.at[1 - c], xres.at[yl], misc.at[1], sib, b_like, root)
        sends.start(xp.at[1 - c], xres.at[1 - yl], misc.at[2], sib, b_like, root)

    @pl.when(leaf)
    def _():
        def pass_on(k, from_pair):
            b6 = fb(yh, at_x[k], c) if from_pair else fb(1 - yh, at_x[k], c)
            got_w(b6, 0)
            send_w(b6, 0, [cross if from_pair else pair], leaf)

        def along_x(y_hi, core, part):
            b5 = fb(y_hi, x, core)
            got_w(b5, part)
            send_w(b5, part, [xs[1], xs[3]], leaf)

        along_x(yh, c, 1)
        along_x(1 - yh, c, 1)
        pass_on(0, True)
        along_x(yh, 1 - c, None)
        along_x(1 - yh, 1 - c, None)
        pass_on(3, False)
        pass_on(1, True)
        pass_on(2, False)

    @pl.when(root)
    def _():
        for y2 in (yl, 1 - yl):
            s1 = at_z[3] * 2 + y2
            got_tok(s1)
            sends.start(tok.at[s1, 0], tok.at[s1, 0], trecv.at[s1], zs[1], b_like, root)
            send_tok(s1, sib, root)
            s2 = at_z[1] * 2 + y2
            got_tok(s2)
            sends.start(tok.at[s2, 1], tok.at[s2, 1], trecv.at[s2], zs[3], b_like, root)
            send_tok(s2, sib, root)

    for yh2 in range(2):
        for core, part in ((c, 1), (1 - c, None)):
            b8 = fb(yh2, at_x[3], core)
            got_w(b8, part)
            b9 = fb(yh2, at_x[1], core)
            got_w(b9, part)
            if yh2 == 0:
                send_w(b8, part, [xs[1]], None)
            else:
                send_w(b9, part, [xs[3]], None)

    p_local.wait()
    rows = (pl.ds(0, 192), pl.ds(192, 192))
    proj_like = pb.at[0, pl.ds(0, 192)]
    for n, to in enumerate((pair, cross)):
        part = pb.at[yl, rows[n]]
        reused.start(part, part, misc.at[3 + n], to, proj_like)

    @pl.when(root)
    def _():
        for k, a, to in ((3, 0, 1), (1, 1, 3)):
            for a2 in range(2):
                got_wt(slot(at_z[k], a2))
            send_wt(slot(at_z[k], a), slot(at_z[k], a), zs[to], root)
        for y2 in (yl, 1 - yl):
            s3 = at_z[2] * 2 + y2
            got_tok(s3)
            send_tok(s3, sib, root)

    pt_local.wait()
    for k in (1, 3, 2):
        sends.start(pt.at[pslot(z)], pt.at[pslot(z)], ptrecv.at[pslot(z)], zs[k], p_like)

    zp = lax.rem(z, 2)

    def to_x(k):
        for a in range(2):
            send_wt(slot(at_x[k], a), fb(yh, x, a), xs[k], root)

    def along_y(k):
        if k:
            for a in range(2):
                got_wt(fb(yh, at_x[k], a))
        b11 = fb(yh, at_x[k], zp)
        send_wt(b11, b11, pair, root)
        send_wt(b11, b11, cross, root)

    def pass_along(k, from_pair):
        b13 = fb(yh if from_pair else 1 - yh, at_x[k], zp)
        got_wt(b13)
        send_wt(b13, b13, cross if from_pair else pair, leaf)

    @pl.when(root)
    def _():
        wt_local.wait()
        for a in range(2):
            got_wt(slot(at_z[2], a))
        to_x(1)
        to_x(3)
        along_y(0)

    @pl.when(root)
    def _():
        for k in range(4):
            got_w(fb(1 - yh, at_x[k], c), 0)
        w_local.wait()
        x_local.wait()
        xp_local.wait()

    @pl.when(leaf)
    def _():
        for s in range(8):
            got_tok(s)
        for k in range(2):
            got_w(fb(yh, at_x[2 + k], c), 0)
            got_w(fb(1 - yh, at_x[k], c), 0)

    for yh2 in range(2):
        for core, part in ((c, 1), (1 - c, None)):
            got_w(fb(yh2, at_x[2], core), part)

    @pl.loop(0, 4)
    def _(i):
        rows4 = tok[pl.ds(2 * i, 2)].reshape(256, D)
        res = jnp.dot(rows4, wb[...].reshape(D, PACK), preferred_element_type=F32)
        qkv[pl.ds(2 * i, 2)] = res.astype(BF16).reshape(2, 2, 64, PACK)

    class Ring:
        def __init__(self, phase, take, at, to):
            self.phase, self.take, self.at, self.to = phase, take, at, to
            self.like = psend.at[phase, 0, 0]

        def term(self, stage, k):
            val = jnp.dot(self.take(stage, 0, self.at[k]), pb[0], preferred_element_type=F32)
            return val + jnp.dot(self.take(stage, 1, self.at[k]), pb[1], preferred_element_type=F32)

        def send(self, stage, n, val, dst, sem, k):
            src = psend.at[self.phase, stage, n]
            src[...] = val.astype(BF16)
            sends.start(src, dst, sem, self.to[k], self.like)

        def relay(self, stage, n):
            return relay.at[self.phase, stage, n], relay_sem.at[self.phase, stage, n]

        def last(self, stage, side, n):
            return rsum.at[self.phase, stage, side, n], rsum_sem.at[self.phase, stage, side, n]

        def begin(self, stage):
            val = self.term(stage, 2)
            self.send(stage, 0, val[:64], *self.relay(stage, 0), 1)
            self.send(stage, 1, val[64:], *self.relay(stage, 1), 3)
            val = self.term(stage, 1)
            self.send(stage, 2, val[64:], *self.last(stage, 0, 1), 1)
            hold[stage, 0] = val[:64]
            val = self.term(stage, 3)
            self.send(stage, 3, val[:64], *self.last(stage, 1, 0), 3)
            hold[stage, 1] = val[64:]
            own[stage] = self.term(stage, 0).reshape(2, 64, HALF)

        def pass_on(self, stage):
            for n, to in ((0, 1), (1, 3)):
                ref, sem = self.relay(stage, n)
                arrived(ref, sem)
                val = hold[stage, n] + ref[...].astype(F32)
                self.send(stage, 4 + n, val, *self.last(stage, n, n), to)

        def end(self, stage):
            for side in range(2):
                for n in range(2):
                    arrived(*self.last(stage, side, n))

        def total(self, stage, n):
            val = own[stage, n] + rsum[self.phase, stage, 0, n].astype(F32)
            return (val + rsum[self.phase, stage, 1, n].astype(F32)).astype(BF16)

    def spatial_heads(i):
        def load(at):
            return qkv[:, i, :, at : at + HEAD].reshape(512, HEAD)

        def store(at, val):
            att[c, i, :, :, at : at + HEAD] = val.reshape(8, 64, HEAD)

        three_heads(load, store, None)
        sends.start(att.at[c, i], att.at[c, i], misc.at[(5, 15)[i]], sib, att.at[0, 0])

    def spatial_heads_there(i):
        arrived(att.at[1 - c, i], misc.at[(5, 15)[i]])

    ring = Ring(
        0,
        lambda stage, core, z2: att[core, stage, pl.ds(2 * z2, 2)].reshape(128, COLS),
        at_z,
        zs,
    )
    spatial_heads(0)

    @pl.when(root)
    def _():
        along_y(1)
        along_y(3)
        to_x(2)

    @pl.when(leaf)
    def _():
        pass_along(0, True)

    for n in range(2):
        part = pb.at[1 - yl, rows[n]]
        arrived(part, misc.at[3 + n])
    spatial_heads_there(0)
    ring.begin(0)
    spatial_heads(1)
    ring.pass_on(0)
    spatial_heads_there(1)
    ring.begin(1)

    @pl.when(root)
    def _():
        along_y(2)

    @pl.when(leaf)
    def _():
        pass_along(3, False)

    ring.pass_on(1)

    @pl.when(leaf)
    def _():
        pass_along(1, True)

    for k in (1, 3, 2):
        got_pt(pslot(at_z[k]))
    for k in (1, 3, 2):
        sends.start(
            pt.at[pslot(at_x[k])], pt.at[yl * 4 + x], ptrecv.at[yl * 4 + x], xs[k], p_like
        )
    reused.finish(sib)

    def fill(n, b, blocks=1):
        at = pl.ds(b, blocks)
        return pltpu.make_async_copy(wt.at[at], wb.at[at], local_sem.at[18 + n])

    @pl.when(root)
    def _():
        fill(0, yh * 8, 8).start()

    n_like = nxt.at[0, pl.ds(0, 32)]

    def piece(y_hi, y_lo):
        return nxt.at[y_lo, pl.ds(pl.multiple_of(y_hi * 32, 32), 32)]

    def t2(y_hi, x_at, y_lo, i):
        return tok2.at[y_hi, x_at, y_lo, i], t2recv.at[fb(y_hi, x_at, y_lo) * 2 + i]

    mine, mine_sem = t2(yh, x, yl, c)
    t2_local = pltpu.make_async_copy(piece(yh, yl), mine, local_sem.at[6])
    lines = ((yh, yl), (yh, 1 - yl), (1 - yh, 1 - yl), (1 - yh, yl))

    def slot_of_patches(y2):
        @pl.loop(0, 4)
        def _(n):
            r = pl.multiple_of(n * 16, 16)
            out = jnp.concatenate([fin[0, y2, pl.ds(r, 16)], fin[1, y2, pl.ds(r, 16)]], axis=-1)
            aft[y2, pl.ds(r, 16)] = out
            val = xres[y2, pl.ds(r, 16)].astype(F32) + gate_ref[0:1] * out.astype(F32)
            val = val.astype(BF16).astype(F32)
            nxt[y2, pl.ds(r, 16)] = normed(val, mod_ref[2:3], mod_ref[3:4])

    def settle(i, here, there):
        ring.end(i)

        @pl.when(there)
        def _():
            for y2 in range(2):
                xch[y2] = ring.total(i, y2)
            sends.start(xch, fin.at[c], misc.at[6], sib, xch, there)

        @pl.when(here)
        def _():
            for y2 in range(2):
                fin[c, y2] = ring.total(i, y2)
            arrived(fin.at[1 - c], misc.at[6])
            slot_of_patches(1 - yl)
            sends.start(piece(yh, 1 - yl), mine, mine_sem, pair, n_like, here)
            sends.start(piece(1 - yh, 1 - yl), mine, mine_sem, cross, n_like, here)
            slot_of_patches(yl)
            for to in (xs[1], xs[3], sib):
                sends.start(piece(yh, yl), mine, mine_sem, to, n_like, here)
            sends.start(piece(1 - yh, yl), mine, mine_sem, far, n_like, here)
            t2_local.start()

    @pl.when(leaf)
    def _():
        arrived(xres.at[0], misc.at[1])
        arrived(xres.at[0], misc.at[2])

    leaf_blocks = ((yh, 0), (1 - yh, 3), (yh, 1), (1 - yh, 2), (yh, 3), (1 - yh, 1), (yh, 2), (1 - yh, 0))

    def along_z(n):
        y_hi, k = leaf_blocks[n]
        b15 = fb(y_hi, at_x[k], zp)
        if n >= 4:
            got_wt(b15)
        send_wt(b15, b15, zs[1 if n % 2 == 0 else 3], leaf)
        fill(n, b15).start()

    core0, core1 = c == 0, c == 1
    settle(0, core0, core1)

    @pl.when(leaf)
    def _():
        for n in range(3):
            along_z(n)
        pass_along(2, False)
        along_z(3)

    settle(1, core1, core0)

    for y2, l2 in lines[1:]:
        dst, sem = t2(y2, x, l2, c)
        arrived(dst, sem)
        for to in (xs[1], xs[3], sib):
            sends.start(dst, dst, sem, to, n_like)


    @pl.when(leaf)
    def _():
        for n in range(4, 8):
            along_z(n)

    @pl.when(root)
    def _():
        for k in range(4):
            b15 = fb(1 - yh, at_x[k], zp)
            got_wt(b15)
            send_wt(b15, b15, zs[1 if k < 2 else 3], root)
            fill(1 + k, b15).start()

    a_like = aft.at[0]
    home_local = pltpu.make_async_copy(aft.at[yl], home.at[c], local_sem.at[7])

    @pl.when(leaf)
    def _():
        sends.start(aft.at[1 - yl], hop, misc.at[7], sib, a_like, leaf)
        sends.start(aft.at[yl], home.at[c], misc.at[8], sib, a_like, leaf)

    @pl.when(root)
    def _():
        home_local.start()

    for n, (y2, l2) in enumerate(lines):
        for k, to in ((3, 1), (1, 3)):
            dst, sem = t2(y2, at_x[k], l2, c)
            arrived(dst, sem)
            if (n < 2) == (k == 3):
                sends.start(dst, dst, sem, xs[to], n_like)
            sends.start(dst, dst, sem, sib, n_like)

    @pl.when(root)
    def _():
        sends.start(aft.at[1 - yl], home.at[c], misc.at[9], pair, a_like, root)
        arrived(hop, misc.at[7])
        sends.start(hop, home.at[1 - c], misc.at[10], pair, a_like, root)

    for k in (1, 3, 2):
        got_pt(yl * 4 + at_x[k])
    for n, to in enumerate((pair, cross)):
        for m in range(2):
            b10 = yl * 4 + 2 * n + m
            sends.start(pt.at[b10], pt.at[b10], ptrecv.at[b10], to, p_like)

    @pl.when(root)
    def _():
        for k in range(4):
            b16 = fb(1 - yh, at_x[k], 1 - zp)
            got_wt(b16)
            fill(5 + k, b16).start()
        fill(0, yh * 8, 8).wait()
        for k in range(4):
            for n, a in ((1 + k, zp), (5 + k, 1 - zp)):
                fill(n, fb(1 - yh, at_x[k], a)).wait()

    @pl.when(leaf)
    def _():
        for n, (y_hi, k) in enumerate(leaf_blocks):
            b16 = fb(y_hi, at_x[k], 1 - zp)
            got_wt(b16)
            fill(8 + n, b16).start()
        for n, (y_hi, k) in enumerate(leaf_blocks):
            for m, a in ((n, zp), (8 + n, 1 - zp)):
                fill(m, fb(y_hi, at_x[k], a)).wait()

    t2_local.wait()

    for k in (0, 3, 1, 2):
        for y2, l2 in lines:
            if k == 2:
                dst, sem = t2(y2, at_x[k], l2, c)
                arrived(dst, sem)
                sends.start(dst, dst, sem, sib, n_like)
        for y2, l2 in lines:
            dst, sem = t2(y2, at_x[k], l2, 1 - c)
            arrived(dst, sem)
        rows4 = tok2[:, pl.ds(at_x[k], 1)].reshape(256, D)
        res = jnp.dot(rows4, wb[...].reshape(D, PACK), preferred_element_type=F32)
        qkv2[:, pl.ds(at_x[k], 1)] = res.astype(BF16).reshape(2, 1, 2, 2, 32, PACK)

    for m in range(4):
        got_pt((1 - yl) * 4 + m)
    p2_local = [
        pltpu.make_async_copy(
            pt.at[m], pb.at[m // 4, pl.ds(96 * (m % 4), 96)], local_sem.at[9 + m]
        )
        for m in range(8)
    ]
    for copy in p2_local:
        copy.start()

    @pl.loop(0, 2)
    def _(i):
        at0 = pl.multiple_of(i * 16, 16)
        same = (
            lax.broadcasted_iota(jnp.int32, (512, 512), 0)
            - lax.broadcasted_iota(jnp.int32, (512, 512), 1)
        ) & 15 == 0

        def load(at):
            return qkv2[:, :, :, :, pl.ds(at0, 16), at : at + HEAD].reshape(512, HEAD)

        def store(at, val):
            att2[c, :, :, :, :, pl.ds(at0, 16), at : at + HEAD] = val.reshape(
                2, 4, 2, 2, 16, HEAD
            )

        three_heads(load, store, same)

    sends.start(att2.at[c], att2.at[c], misc.at[11], sib, att2.at[0])

    @pl.when(leaf)
    def _():
        arrived(home.at[0], misc.at[9])
        arrived(home.at[0], misc.at[10])

    @pl.when(root)
    def _():
        home_local.wait()
        arrived(home.at[0], misc.at[8])

    after_local = pltpu.make_async_copy(home, after_ref, local_sem.at[17])
    after_local.start()
    for copy in p2_local:
        copy.wait()
    arrived(att2.at[1 - c], misc.at[11])

    ring = Ring(
        1,
        lambda stage, core, x2: att2[core, yh if stage else 1 - yh, x2].reshape(128, COLS),
        at_x,
        xs,
    )
    ring.begin(0)
    ring.pass_on(0)
    ring.begin(1)
    ring.pass_on(1)

    def collect(stage, y2):
        ring.end(stage)
        for l2 in range(2):
            fin2[y2, l2, c] = ring.total(stage, l2).reshape(2, 32, HALF)
        part = fin2.at[y2, 1 - c, c]
        sends.start(part, part, misc.at[12 + stage], sib, fin2.at[0, 0, 0])

    collect(0, 1 - yh)
    arrived(fin2.at[1 - yh, c, 1 - c], misc.at[12])
    sends.start(fin2.at[1 - yh, c], hb, misc.at[14], far, hb)
    collect(1, yh)
    arrived(fin2.at[yh, c, 1 - c], misc.at[13])

    def finish(part, tiles):
        at = pl.ds(pl.multiple_of(part * 32, 32), 32)
        for i in range(2):
            out_ref[i, at] = jnp.concatenate([tiles[0][i], tiles[1][i]], axis=-1)

    finish(yh, [fin2[yh, c, n] for n in range(2)])
    arrived(hb, misc.at[14])
    finish(1 - yh, [hb[n] for n in range(2)])
    after_local.wait()
    sends.finish(sib)


VMEM = pl.BlockSpec(memory_space=pltpu.VMEM)
ANY = pl.BlockSpec(memory_space=pl.ANY)
HBM = pl.BlockSpec(memory_space=pltpu.HBM)


def local(*args):
    block = jax.ShapeDtypeStruct((2, 64, D), BF16)

    def buffer(*shape, dtype=BF16):
        return pltpu.VMEM(shape, dtype)

    def sems(*shape):
        return pltpu.SemaphoreType.DMA(shape)

    outs = pl.pallas_call(
        kernel,
        out_shape=(
            block,
            block,
            jax.ShapeDtypeStruct((24, 192, PACK), BF16),
            jax.ShapeDtypeStruct((12, 96, HALF), BF16),
        ),
        in_specs=[VMEM, VMEM, VMEM, VMEM, ANY, VMEM, VMEM, VMEM, ANY, VMEM, VMEM],
        out_specs=(VMEM, VMEM, HBM, HBM),
        scratch_shapes=[
            buffer(2, 64, D),
            buffer(192, PACK),
            buffer(192, PACK),
            buffer(8, 2, 64, D),
            buffer(2, 4, 2, 2, 32, D),
            buffer(16, 192, PACK),
            buffer(2, COLS, HALF),
            buffer(8, 2, 64, PACK),
            buffer(2, 4, 2, 2, 32, PACK),
            buffer(2, 2, 8, 64, COLS),
            buffer(2, 2, 4, 2, 2, 32, COLS),
            buffer(2, 2, 6, 64, HALF),
            buffer(2, 2, 2, 64, HALF),
            buffer(2, 2, 2, 2, 64, HALF),
            buffer(2, 2, 64, HALF, dtype=F32),
            buffer(2, 2, 64, HALF, dtype=F32),
            buffer(2, 2, 64, HALF),
            buffer(2, 64, D),
            buffer(2, 64, D),
            buffer(2, 64, D),
            buffer(2, 64, D),
            buffer(64, D),
            buffer(2, 64, HALF),
            buffer(2, 2, 2, 2, 32, HALF),
            buffer(2, 2, 32, HALF),
            sems(288),
            sems(8),
            sems(32),
            sems(24),
            sems(12),
            sems(32),
            sems(2, 2, 2),
            sems(2, 2, 2, 2),
            sems(16),
            sems(34),
        ],
        compiler_params=pltpu.CompilerParams(
            collective_id=1, has_side_effects=True, vmem_limit_bytes=63 << 20
        ),
        cost_estimate=pl.CostEstimate(
            flops=24 * 10**9, bytes_accessed=200 << 20, transcendentals=1 << 22
        ),
        name="sublayers",
    )(*args)
    tokens, gates = args[0].astype(F32), args[10]
    after_spatial = (tokens + gates[0] * outs[0].astype(F32)).astype(BF16)
    after_temporal = (after_spatial.astype(F32) + gates[1] * outs[1].astype(F32)).astype(BF16)
    return after_spatial, after_temporal


def solution(mesh):
    placed = (
        P("frame", "patch", None),
        P("frame", "patch"),
        P("frame", "patch"),
        P("frame", "patch"),
        P("patch", None),
        P("frame", "patch"),
        P("frame", "patch"),
        P("frame", "patch"),
        P("patch", None),
        P(),
        P(),
    )
    return jax.shard_map(
        local,
        mesh=mesh,
        in_specs=placed,
        out_specs=(P("frame", "patch", None), P("frame", "patch", None)),
        check_vma=False,
    )
```
